512 devices in a mesh: span: 4 (over y_lo), head: 8 (over x, core), seq: 16 (over z, y_hi).
Axes of the slice: x: 4, y: 8 (y_hi: 2, y_lo: 4; y = y_hi * 4 + y_lo), z: 8, core: 2. Of those that a mesh axis runs over, the one named last changes fastest.
Arguments:
- queries: bfloat16 [3072, 5120], P(('span', 'seq'), 'head'), may hold values from -8 to 8
- keys: bfloat16 [3072, 5120], P(('span', 'seq'), 'head'), may hold values from -8 to 8
- values: bfloat16 [3072, 5120], P(('span', 'seq'), 'head'), may hold values from -6 to 6
- out_weight: bfloat16 [5120, 5120], P('head', 'seq'), may hold values from -0.078125 to 0.078125
- gate_table: float32 [50, 5120], P(None, 'seq'), may hold values from 0.25 to 2
- noise_level: int32 [4], replicated, may hold values from 0 to 49
- span_order: int32 [4], replicated, may hold values from 0 to 3, each once
Outputs:
- branch: bfloat16 [3072, 5120], P(('span', 'head'), 'seq')
The draws below stay inside these ranges and needn't reach their ends.
All inputs are finite; a program needn't handle non-finite values.
Results may differ from the reference program's by a relative error of at most 0.035.
Values may be sent and summed in bfloat16 or wider, within the bound.
No kernel may reach another device: no remote copies, remote signals or barrier semaphores. Data moves between devices by JAX's collectives and lax.ppermute only.
A program may use at most 64 MiB of HBM per device.

```python
import math
import jax
import jax.numpy as jnp
from jax import lax

D = 5120
HEADS = 40
HEAD_DIM = 128
LEVELS = 50
SPANS = 4
SPAN_TOKENS = 768
TOKENS = 3072


def draw_queries(key, part):
    key = jax.random.fold_in(key, 1)
    drawn = jnp.clip(2.0 * jax.random.normal(key, (TOKENS, HEADS * HEAD_DIM)), -8.0, 8.0)
    return drawn.astype(jnp.bfloat16)


def draw_keys(key, part):
    key = jax.random.fold_in(key, 2)
    drawn = jnp.clip(2.0 * jax.random.normal(key, (TOKENS, HEADS * HEAD_DIM)), -8.0, 8.0)
    return drawn.astype(jnp.bfloat16)


def touch_ends(entries, key, least, high):
    spot = [jax.random.randint(jax.random.fold_in(key, axis), (), 0, length) for axis, length in enumerate(entries.shape)]
    longest = entries.shape.index(max(entries.shape))
    next_to = spot[:longest] + [(spot[longest] + 1) % entries.shape[longest]] + spot[longest + 1:]
    return entries.at[tuple(spot)].set(least).at[tuple(next_to)].set(high)


def block_scale(own_key, extent, cuts, low, high):
    factor_of = 1.0
    for axis_at, blocks in cuts:
        steps = jax.random.uniform(jax.random.fold_in(jax.random.fold_in(own_key, 6), axis_at), (blocks,), jnp.float32, low / len(cuts), high / len(cuts))
        factor_of = factor_of * jnp.repeat(jnp.exp(steps), extent[axis_at] // blocks).reshape((-1,) + (1,) * (len(extent) - 1 - axis_at))
    return factor_of


def centred(own_key, shape, spread, bound, pieces=(), kind=jnp.bfloat16):
    entries = jax.random.normal(own_key, shape, jnp.float32) * spread
    if len(pieces) > 0:
        entries = block_scale(own_key, shape, pieces, -0.22, 0.18) * entries
    return jnp.clip(entries, min=-bound, max=bound).astype(kind)


def setup_inputs(seed: int = 0) -> dict:
    key_of = jax.random.split(jax.random.key(seed), 8)
    return {
        "queries": draw_queries(jax.random.fold_in(key_of[7], 71), 0),
        "keys": draw_keys(jax.random.fold_in(key_of[7], 71), 0),
        "values": centred(key_of[2], (TOKENS, HEADS * HEAD_DIM), 1.0, 6.0, ((0, 64), (1, 8))),
        "out_weight": centred(key_of[3], (HEADS * HEAD_DIM, D), (HEADS * HEAD_DIM) ** -0.5, 0.078125, ((0, 8), (1, 16))),
        "gate_table": jnp.clip(0.25 + 1.75 * jax.random.uniform(key_of[4], (LEVELS, D), jnp.float32) ** block_scale(key_of[4], (LEVELS, D), ((1, 16),), -0.2, 0.2), 0.25, 2.0),
        "noise_level": touch_ends(jax.random.randint(key_of[5], (SPANS,), 0, LEVELS), jax.random.fold_in(key_of[5], 1), 0, LEVELS - 1).astype(jnp.int32),
        "span_order": jax.random.permutation(key_of[6], SPANS).astype(jnp.int32),
    }


def attend_head(query_head, key_head, value_head, visible, scale):
    scores = jnp.dot(query_head, key_head.T, preferred_element_type=jnp.float32) * scale
    scores = jnp.where(visible[None, :], scores, -jnp.inf)
    highest = lax.optimization_barrier(jnp.max(scores, axis=1, keepdims=True))
    weights = jnp.exp(scores - highest)
    total = lax.optimization_barrier(jnp.sum(weights, axis=1, keepdims=True))
    mixed = jnp.dot(weights.astype(jnp.bfloat16), value_head, preferred_element_type=jnp.float32)
    return (mixed / total).astype(jnp.bfloat16)

def reference(queries, keys, values, out_weight, gate_table, noise_level, span_order):
    width = HEADS * HEAD_DIM
    scale = 1.0 / math.sqrt(HEAD_DIM)
    key_heads = keys.reshape(TOKENS, HEADS, HEAD_DIM).transpose(1, 0, 2)
    value_heads = values.reshape(TOKENS, HEADS, HEAD_DIM).transpose(1, 0, 2)
    query_blocks = queries.reshape(SPANS, SPAN_TOKENS, HEADS, HEAD_DIM).transpose(0, 2, 1, 3)
    key_place = jnp.repeat(span_order, SPAN_TOKENS)

    def one_span(entry):
        query_block, position = entry
        visible = key_place <= position

        def one_head(triple):
            return attend_head(triple[0], triple[1], triple[2], visible, scale)
        return lax.map(one_head, (query_block, key_heads, value_heads))
    attended = lax.map(one_span, (query_blocks, span_order))
    attended = attended.transpose(0, 2, 1, 3).reshape(TOKENS, width)
    projected = jnp.dot(attended, out_weight, preferred_element_type=jnp.float32)
    gates = gate_table[noise_level]
    branch = projected.reshape(SPANS, SPAN_TOKENS, D) * gates[:, None, :]
    return branch.reshape(TOKENS, D).astype(jnp.bfloat16)
```

```python
import functools
import math

import jax
import jax.numpy as jnp
from jax import lax
from jax.experimental import pallas as pl
from jax.experimental.pallas import tpu as pltpu
from jax.sharding import PartitionSpec as P

HEAD_DIM = 128
SPANS = 4
GROUPS = 8
HEADS_HERE = 5
BLOCKS = 3
PLACES = 16
ROWS = 48
QROWS = ROWS // BLOCKS
SPAN_ROWS = PLACES * ROWS
QBLOCK = PLACES * QROWS
PIECE = QBLOCK // GROUPS
STATS = 8
HIDDEN = -1.0e30
EXP2_SCALE = math.log2(math.e) / math.sqrt(HEAD_DIM)
VMEM = pl.BlockSpec(memory_space=pltpu.VMEM)
SMEM = pl.BlockSpec(memory_space=pltpu.SMEM)


def params(mib=24):
    return pltpu.CompilerParams(vmem_limit_bytes=mib * 2**20)


def pack_kernel(q_ref, k_ref, v_ref, out_ref):
    for head in range(HEADS_HERE):
        cols = slice(head * HEAD_DIM, (head + 1) * HEAD_DIM)
        key_rows = k_ref[:, cols]
        value_rows = v_ref[:, cols]
        for block in range(BLOCKS):
            place = head * BLOCKS + block
            out_ref[place, :QROWS, :] = q_ref[block * QROWS : (block + 1) * QROWS, cols]
            out_ref[place, QROWS : QROWS + ROWS, :] = key_rows
            out_ref[place, QROWS + ROWS :, :] = value_rows
    for place in range(HEADS_HERE * BLOCKS, PLACES):
        out_ref[place] = jnp.zeros(out_ref.shape[1:], out_ref.dtype)


def split_three(x):
    high = x.astype(jnp.bfloat16)
    rest = x - high.astype(jnp.float32)
    middle = rest.astype(jnp.bfloat16)
    low = (rest - middle.astype(jnp.float32)).astype(jnp.bfloat16)
    return high, middle, low


def attend_kernel(order_ref, me_ref, rows_ref, q_ref, out_ref):
    my_place = order_ref[me_ref[0]]
    keys = rows_ref[:, QROWS : QROWS + ROWS, :].reshape(SPAN_ROWS, HEAD_DIM)
    values = rows_ref[:, QROWS + ROWS :, :].reshape(SPAN_ROWS, HEAD_DIM)

    for span in range(SPANS):
        seen = my_place <= order_ref[span]

        @pl.when(seen)
        def _():
            scores = lax.dot_general(
                q_ref[span], keys, (((1,), (1,)), ((), ())), preferred_element_type=jnp.float32
            )
            scores = scores * EXP2_SCALE
            highest = jnp.max(scores, axis=1, keepdims=True)
            weights = jnp.exp2(scores - highest)
            total = jnp.sum(weights, axis=1, keepdims=True)
            mixed = jnp.dot(
                weights.astype(jnp.bfloat16), values, preferred_element_type=jnp.float32
            )
            mixed = (mixed / total).astype(jnp.bfloat16)
            logsum = highest + jnp.log2(total)
            wide = jnp.transpose(jnp.broadcast_to(logsum, (QBLOCK, HEAD_DIM)))
            terms = split_three(wide[:STATS])
            for group in range(GROUPS):
                piece = span * GROUPS + group
                out_ref[piece, :PIECE, :] = mixed[group * PIECE : (group + 1) * PIECE]
                half = group * PIECE // HEAD_DIM
                lanes = slice(half * HEAD_DIM, (half + 1) * HEAD_DIM)
                which = lax.broadcasted_iota(jnp.int32, (STATS, HEAD_DIM), 0)
                high, middle, low = (t[:, lanes].astype(jnp.float32) for t in terms)
                stat = jnp.where(which == 0, high, jnp.where(which == 1, middle, low))
                out_ref[piece, PIECE:, :] = stat.astype(jnp.bfloat16)

        @pl.when(jnp.logical_not(seen))
        def _():
            for group in range(GROUPS):
                piece = span * GROUPS + group
                out_ref[piece, :PIECE, :] = jnp.zeros((PIECE, HEAD_DIM), jnp.bfloat16)
                out_ref[piece, PIECE:, :] = jnp.full((STATS, HEAD_DIM), HIDDEN, jnp.bfloat16)


def merge_kernel(group_ref, parts_ref, out_ref, turn_ref):
    stats = parts_ref[:, PIECE:, :].astype(jnp.float32)
    logsum = stats[:, 0, :] + stats[:, 1, :] + stats[:, 2, :]
    pad = jnp.zeros((HEAD_DIM - SPANS * GROUPS, HEAD_DIM), jnp.float32)
    turn_ref[...] = jnp.transpose(jnp.concatenate([logsum, pad], axis=0))
    begin = lax.rem(group_ref[0], HEAD_DIM // PIECE) * PIECE
    mine = turn_ref[pl.ds(pl.multiple_of(begin, PIECE), PIECE), :]
    for group in range(GROUPS):
        cols = [mine[:, s * GROUPS + group : s * GROUPS + group + 1] for s in range(SPANS)]
        highest = functools.reduce(jnp.maximum, cols)
        shares = [jnp.exp2(c - highest) for c in cols]
        total = functools.reduce(jnp.add, shares)
        mixed = jnp.zeros((PIECE, HEAD_DIM), jnp.float32)
        for s in range(SPANS):
            part = parts_ref[s * GROUPS + group, :PIECE, :].astype(jnp.float32)
            mixed = mixed + part * (shares[s] / total)
        mixed = mixed.astype(jnp.bfloat16)
        for place in range(PLACES):
            out_ref[place, :, group * HEAD_DIM : (group + 1) * HEAD_DIM] = mixed


def project_kernel(level_ref, rows_ref, weight_ref, gate_ref, out_ref):
    acc = jnp.zeros((BLOCKS * PIECE, out_ref.shape[1]), jnp.float32)
    width = HEADS_HERE * HEAD_DIM
    for head in range(HEADS_HERE):
        for pair in range(GROUPS // 2):
            lanes = slice(2 * pair * HEAD_DIM, 2 * (pair + 1) * HEAD_DIM)
            left = jnp.concatenate(
                [rows_ref[head * BLOCKS + b, :, lanes] for b in range(BLOCKS)], axis=0
            )
            first = 2 * pair * width + head * HEAD_DIM
            right = jnp.concatenate(
                [
                    weight_ref[first : first + HEAD_DIM, :],
                    weight_ref[first + width : first + width + HEAD_DIM, :],
                ],
                axis=0,
            )
            acc = acc + jnp.dot(left, right, preferred_element_type=jnp.float32)
    gated = (acc * gate_ref[pl.ds(level_ref[0], 1), :]).astype(jnp.bfloat16)
    for block in range(BLOCKS):
        for side in range(2):
            source = block * PIECE + side * QROWS
            target = side * ROWS + block * QROWS
            out_ref[target : target + QROWS, :] = gated[source : source + QROWS]


def shards(queries, keys, values, out_weight, gate_table, noise_level, span_order):
    my_span = lax.axis_index("span")
    my_group = lax.axis_index("head")
    weight = lax.all_gather(out_weight, "head", axis=0, tiled=True)
    packed = pl.pallas_call(
        pack_kernel,
        out_shape=jax.ShapeDtypeStruct((PLACES, QROWS + 2 * ROWS, HEAD_DIM), jnp.bfloat16),
        in_specs=[VMEM] * 3,
        out_specs=VMEM,
        compiler_params=params(),
        name="pack",
    )(queries, keys, values)
    rows = lax.all_to_all(packed, "seq", 0, 0, tiled=True)
    own = rows[:, :QROWS, :].reshape(QBLOCK, HEAD_DIM)
    q_all = lax.all_gather(own, "span", axis=0, tiled=False)
    parts = pl.pallas_call(
        attend_kernel,
        out_shape=jax.ShapeDtypeStruct((SPANS * GROUPS, PIECE + STATS, HEAD_DIM), jnp.bfloat16),
        in_specs=[SMEM, SMEM, VMEM, VMEM],
        out_specs=VMEM,
        compiler_params=params(),
        name="attend",
    )(span_order, my_span.reshape(1), rows, q_all)
    parts = lax.all_to_all(parts, ("span", "head"), 0, 0, tiled=True)
    merged = pl.pallas_call(
        merge_kernel,
        out_shape=jax.ShapeDtypeStruct((PLACES, PIECE, GROUPS * HEAD_DIM), jnp.bfloat16),
        in_specs=[SMEM, VMEM],
        out_specs=VMEM,
        scratch_shapes=[pltpu.VMEM((HEAD_DIM, HEAD_DIM), jnp.float32)],
        compiler_params=params(),
        name="merge",
    )(my_group.reshape(1), parts)
    merged = lax.all_to_all(merged, "seq", 0, 0, tiled=True)
    level = lax.dynamic_slice(noise_level, (my_span,), (1,))
    return pl.pallas_call(
        project_kernel,
        out_shape=jax.ShapeDtypeStruct((BLOCKS * PIECE, out_weight.shape[1]), jnp.bfloat16),
        in_specs=[SMEM, VMEM, VMEM, VMEM],
        out_specs=VMEM,
        compiler_params=params(),
        name="project",
    )(level, merged, weight, gate_table)


def solution(mesh):
    return jax.shard_map(
        shards,
        mesh=mesh,
        in_specs=(
            P(("span", "seq"), "head"),
            P(("span", "seq"), "head"),
            P(("span", "seq"), "head"),
            P("head", "seq"),
            P(None, "seq"),
            P(),
            P(),
        ),
        out_specs=P(("span", "head"), "seq"),
        check_vma=False,
    )
```

```python
import functools
import math

import jax
import jax.numpy as jnp
from jax import lax
from jax.experimental import pallas as pl
from jax.experimental.pallas import tpu as pltpu
from jax.sharding import PartitionSpec as P

HEAD_DIM = 128
SPANS = 4
GROUPS = 8
HEADS_HERE = 5
BLOCKS = 3
PLACES = 16
ROWS = 48
QROWS = ROWS // BLOCKS
KROWS = ROWS // SPANS
KBLOCK = PLACES * KROWS
QBLOCK = PLACES * QROWS
PIECE = QBLOCK // GROUPS
STATS = 8
EXP2_SCALE = math.log2(math.e) / math.sqrt(HEAD_DIM)
VMEM = pl.BlockSpec(memory_space=pltpu.VMEM)
ANY = pl.BlockSpec(memory_space=pl.ANY)
SMEM = pl.BlockSpec(memory_space=pltpu.SMEM)


def params(mib=24):
    return pltpu.CompilerParams(vmem_limit_bytes=mib * 2**20)


def pack_kernel(q_hbm, k_hbm, v_hbm, out_ref, q_ref, k_ref, v_ref, kv_ref, sems):
    copies = [
        pltpu.make_async_copy(source, target, sems.at[i])
        for i, (source, target) in enumerate(((q_hbm, q_ref), (k_hbm, k_ref), (v_hbm, v_ref)))
    ]
    for copy in copies:
        copy.start()
    for span in range(SPANS):
        for place in range(HEADS_HERE * BLOCKS, PLACES):
            out_ref[span * PLACES + place] = jnp.zeros(out_ref.shape[1:], out_ref.dtype)
    copies[0].wait()
    for head in range(HEADS_HERE):
        cols = slice(head * HEAD_DIM, (head + 1) * HEAD_DIM)
        for block in range(BLOCKS):
            part = q_ref[block * QROWS : (block + 1) * QROWS, cols]
            for span in range(SPANS):
                out_ref[span * PLACES + head * BLOCKS + block, :QROWS, :] = part
    copies[1].wait()
    copies[2].wait()
    key_rows = k_ref[...].astype(jnp.float32)
    value_rows = v_ref[...].astype(jnp.float32)
    for span in range(SPANS):
        kv_ref[span, :KROWS, :] = key_rows[span * KROWS : (span + 1) * KROWS]
        kv_ref[span, KROWS:, :] = value_rows[span * KROWS : (span + 1) * KROWS]
    for span in range(SPANS):
        both = kv_ref[span].astype(jnp.bfloat16)
        for head in range(HEADS_HERE):
            part = both[:, head * HEAD_DIM : (head + 1) * HEAD_DIM]
            for block in range(BLOCKS):
                out_ref[span * PLACES + head * BLOCKS + block, QROWS:, :] = part


def split_three(x):
    high = x.astype(jnp.bfloat16)
    rest = x - high.astype(jnp.float32)
    middle = rest.astype(jnp.bfloat16)
    low = (rest - middle.astype(jnp.float32)).astype(jnp.bfloat16)
    return high, middle, low


def attend_kernel(order_ref, rows_ref, out_ref, keys_ref, values_ref):
    which = lax.broadcasted_iota(jnp.int32, (STATS, HEAD_DIM), 0)
    for turn in range(SPANS):
        span = jnp.int32(0)
        for other in range(1, SPANS):
            span = span + jnp.where(order_ref[other] == turn, other, 0)
        first = span * PLACES
        for place in range(PLACES):
            both = rows_ref[first + place, QROWS:, :].astype(jnp.float32)
            target = turn * KBLOCK + place * KROWS
            keys_ref[target : target + KROWS, :] = both[:KROWS]
            values_ref[target : target + KROWS, :] = both[KROWS:]
        seen = (turn + 1) * KBLOCK
        keys = keys_ref[:seen, :].astype(jnp.bfloat16)
        values = values_ref[:seen, :].astype(jnp.bfloat16)
        own = rows_ref[pl.ds(first, PLACES), :QROWS, :].reshape(QBLOCK, HEAD_DIM)
        scores = lax.dot_general(
            own, keys, (((1,), (1,)), ((), ())), preferred_element_type=jnp.float32
        )
        scores = scores * EXP2_SCALE
        highest = jnp.max(scores, axis=1, keepdims=True)
        weights = jnp.exp2(scores - highest)
        total = jnp.sum(weights, axis=1, keepdims=True)
        mixed = jnp.dot(weights.astype(jnp.bfloat16), values, preferred_element_type=jnp.float32)
        mixed = (mixed / total).astype(jnp.bfloat16)
        logsum = highest + jnp.log2(total)
        wide = jnp.transpose(jnp.broadcast_to(logsum, (QBLOCK, HEAD_DIM)))
        high, middle, low = (t.astype(jnp.float32) for t in split_three(wide[:STATS]))
        for group in range(GROUPS):
            half = group * PIECE // HEAD_DIM
            lanes = slice(half * HEAD_DIM, (half + 1) * HEAD_DIM)
            stat = jnp.where(
                which == 0, high[:, lanes], jnp.where(which == 1, middle[:, lanes], low[:, lanes])
            )
            piece = span * GROUPS + group
            out_ref[piece, :PIECE, :] = mixed[group * PIECE : (group + 1) * PIECE]
            out_ref[piece, PIECE:, :] = stat.astype(jnp.bfloat16)


def merge_kernel(group_ref, parts_ref, out_ref, turn_ref):
    stats = parts_ref[:, PIECE:, :].astype(jnp.float32)
    logsum = stats[:, 0, :] + stats[:, 1, :] + stats[:, 2, :]
    pad = jnp.zeros((HEAD_DIM - SPANS * GROUPS, HEAD_DIM), jnp.float32)
    turn_ref[...] = jnp.transpose(jnp.concatenate([logsum, pad], axis=0))
    begin = lax.rem(group_ref[0], HEAD_DIM // PIECE) * PIECE
    mine = turn_ref[pl.ds(pl.multiple_of(begin, PIECE), PIECE), :]
    for group in range(GROUPS):
        cols = [mine[:, s * GROUPS + group : s * GROUPS + group + 1] for s in range(SPANS)]
        highest = functools.reduce(jnp.maximum, cols)
        shares = [jnp.exp2(c - highest) for c in cols]
        total = functools.reduce(jnp.add, shares)
        mixed = jnp.zeros((PIECE, HEAD_DIM), jnp.float32)
        for s in range(SPANS):
            part = parts_ref[s * GROUPS + group, :PIECE, :].astype(jnp.float32)
            mixed = mixed + part * (shares[s] / total)
        mixed = mixed.astype(jnp.bfloat16)
        for place in range(PLACES):
            out_ref[place, :, group * HEAD_DIM : (group + 1) * HEAD_DIM] = mixed


def project_kernel(level_ref, rows_ref, weight_ref, gate_ref, out_ref):
    acc = jnp.zeros((BLOCKS * PIECE, out_ref.shape[1]), jnp.float32)
    for head in range(HEADS_HERE):
        for pair in range(GROUPS // 2):
            lanes = slice(2 * pair * HEAD_DIM, 2 * (pair + 1) * HEAD_DIM)
            left = jnp.concatenate(
                [rows_ref[head * BLOCKS + b, :, lanes] for b in range(BLOCKS)], axis=0
            )
            mine = slice(head * HEAD_DIM, (head + 1) * HEAD_DIM)
            right = jnp.concatenate(
                [weight_ref[2 * pair, :, mine], weight_ref[2 * pair + 1, :, mine]], axis=1
            )
            acc = acc + lax.dot_general(
                left, right, (((1,), (1,)), ((), ())), preferred_element_type=jnp.float32
            )
    gated = (acc * gate_ref[pl.ds(level_ref[0], 1), :]).astype(jnp.bfloat16)
    for block in range(BLOCKS):
        for side in range(2):
            source = block * PIECE + side * QROWS
            target = side * ROWS + block * QROWS
            out_ref[target : target + QROWS, :] = gated[source : source + QROWS]


def shards(queries, keys, values, out_weight, gate_table, noise_level, span_order):
    my_span = lax.axis_index("span")
    my_group = lax.axis_index("head")
    weight = lax.all_gather(out_weight.T, "head", axis=0, tiled=False)
    shard = (ROWS, HEADS_HERE * HEAD_DIM)
    packed = pl.pallas_call(
        pack_kernel,
        out_shape=jax.ShapeDtypeStruct((SPANS * PLACES, QROWS + 2 * KROWS, HEAD_DIM), jnp.bfloat16),
        in_specs=[ANY] * 3,
        out_specs=VMEM,
        scratch_shapes=[pltpu.VMEM(shard, jnp.bfloat16)] * 3
        + [
            pltpu.VMEM((SPANS, 2 * KROWS, shard[1]), jnp.float32),
            pltpu.SemaphoreType.DMA((3,)),
        ],
        compiler_params=params(),
        name="pack",
    )(queries, keys, values)
    rows = lax.all_to_all(packed, ("span", "seq"), 0, 0, tiled=True)
    parts = pl.pallas_call(
        attend_kernel,
        out_shape=jax.ShapeDtypeStruct((SPANS * GROUPS, PIECE + STATS, HEAD_DIM), jnp.bfloat16),
        in_specs=[SMEM, VMEM],
        out_specs=VMEM,
        scratch_shapes=[pltpu.VMEM((SPANS * KBLOCK, HEAD_DIM), jnp.float32)] * 2,
        compiler_params=params(),
        name="attend",
    )(span_order, rows)
    parts = lax.all_to_all(parts, ("span", "head"), 0, 0, tiled=True)
    parts, weight = lax.optimization_barrier((parts, weight))
    merged = pl.pallas_call(
        merge_kernel,
        out_shape=jax.ShapeDtypeStruct((PLACES, PIECE, GROUPS * HEAD_DIM), jnp.bfloat16),
        in_specs=[SMEM, VMEM],
        out_specs=VMEM,
        scratch_shapes=[pltpu.VMEM((HEAD_DIM, HEAD_DIM), jnp.float32)],
        compiler_params=params(),
        name="merge",
    )(my_group.reshape(1), parts)
    merged = lax.all_to_all(merged, "seq", 0, 0, tiled=True)
    level = lax.dynamic_slice(noise_level, (my_span,), (1,))
    return pl.pallas_call(
        project_kernel,
        out_shape=jax.ShapeDtypeStruct((BLOCKS * PIECE, out_weight.shape[1]), jnp.bfloat16),
        in_specs=[SMEM, VMEM, VMEM, VMEM],
        out_specs=VMEM,
        compiler_params=params(),
        name="project",
    )(level, merged, weight, gate_table)


def solution(mesh):
    return jax.shard_map(
        shards,
        mesh=mesh,
        in_specs=(
            P(("span", "seq"), "head"),
            P(("span", "seq"), "head"),
            P(("span", "seq"), "head"),
            P("head", "seq"),
            P(None, "seq"),
            P(),
            P(),
        ),
        out_specs=P(("span", "head"), "seq"),
        check_vma=False,
    )
```

```python
import functools
import math

import jax
import jax.numpy as jnp
from jax import lax
from jax.experimental import pallas as pl
from jax.experimental.pallas import tpu as pltpu
from jax.sharding import PartitionSpec as P

HEAD_DIM = 128
SPANS = 4
RING, CORES = 4, 2
GROUPS = 8
HEADS_HERE = 5
BLOCKS = 3
PLACES = 16
ROWS = 48
QROWS = ROWS // BLOCKS
KROWS = ROWS // SPANS
KBLOCK = PLACES * KROWS
QBLOCK = PLACES * QROWS
PIECE = QBLOCK // GROUPS
STATS = 8
EXP2_SCALE = math.log2(math.e) / math.sqrt(HEAD_DIM)
VMEM = pl.BlockSpec(memory_space=pltpu.VMEM)
HBM = pl.BlockSpec(memory_space=pltpu.HBM)
SMEM = pl.BlockSpec(memory_space=pltpu.SMEM)


def params(mib=24):
    return pltpu.CompilerParams(vmem_limit_bytes=mib * 2**20)


def pack_kernel(q_hbm, k_hbm, v_hbm, out_ref, q_ref, k_ref, v_ref, kv_ref, sems):
    copies = [
        pltpu.make_async_copy(source, target, sems.at[i])
        for i, (source, target) in enumerate(((q_hbm, q_ref), (k_hbm, k_ref), (v_hbm, v_ref)))
    ]
    for copy in copies:
        copy.start()
    for span in range(SPANS):
        for place in range(HEADS_HERE * BLOCKS, PLACES):
            out_ref[span * PLACES + place] = jnp.zeros(out_ref.shape[1:], out_ref.dtype)
    copies[0].wait()
    for head in range(HEADS_HERE):
        cols = slice(head * HEAD_DIM, (head + 1) * HEAD_DIM)
        for block in range(BLOCKS):
            part = q_ref[block * QROWS : (block + 1) * QROWS, cols]
            for span in range(SPANS):
                out_ref[span * PLACES + head * BLOCKS + block, :QROWS, :] = part
    copies[1].wait()
    copies[2].wait()
    key_rows = k_ref[...].astype(jnp.float32)
    value_rows = v_ref[...].astype(jnp.float32)
    for span in range(SPANS):
        kv_ref[span, :KROWS, :] = key_rows[span * KROWS : (span + 1) * KROWS]
        kv_ref[span, KROWS:, :] = value_rows[span * KROWS : (span + 1) * KROWS]
    for span in range(SPANS):
        both = kv_ref[span].astype(jnp.bfloat16)
        for head in range(HEADS_HERE):
            part = both[:, head * HEAD_DIM : (head + 1) * HEAD_DIM]
            for block in range(BLOCKS):
                out_ref[span * PLACES + head * BLOCKS + block, QROWS:, :] = part


def split_three(x):
    high = x.astype(jnp.bfloat16)
    rest = x - high.astype(jnp.float32)
    middle = rest.astype(jnp.bfloat16)
    low = (rest - middle.astype(jnp.float32)).astype(jnp.bfloat16)
    return high, middle, low


def attend_kernel(order_ref, rows_ref, out_ref, keys_ref, values_ref):
    which = lax.broadcasted_iota(jnp.int32, (STATS, HEAD_DIM), 0)
    for turn in range(SPANS):
        span = jnp.int32(0)
        for other in range(1, SPANS):
            span = span + jnp.where(order_ref[other] == turn, other, 0)
        first = span * PLACES
        for place in range(PLACES):
            both = rows_ref[first + place, QROWS:, :].astype(jnp.float32)
            target = turn * KBLOCK + place * KROWS
            keys_ref[target : target + KROWS, :] = both[:KROWS]
            values_ref[target : target + KROWS, :] = both[KROWS:]
        seen = (turn + 1) * KBLOCK
        keys = keys_ref[:seen, :].astype(jnp.bfloat16)
        values = values_ref[:seen, :].astype(jnp.bfloat16)
        own = rows_ref[pl.ds(first, PLACES), :QROWS, :].reshape(QBLOCK, HEAD_DIM)
        scores = lax.dot_general(
            own, keys, (((1,), (1,)), ((), ())), preferred_element_type=jnp.float32
        )
        scores = scores * EXP2_SCALE
        highest = jnp.max(scores, axis=1, keepdims=True)
        weights = jnp.exp2(scores - highest)
        total = jnp.sum(weights, axis=1, keepdims=True)
        mixed = jnp.dot(weights.astype(jnp.bfloat16), values, preferred_element_type=jnp.float32)
        mixed = (mixed / total).astype(jnp.bfloat16)
        logsum = highest + jnp.log2(total)
        wide = jnp.transpose(jnp.broadcast_to(logsum, (QBLOCK, HEAD_DIM)))
        high, middle, low = (t.astype(jnp.float32) for t in split_three(wide[:STATS]))
        for group in range(GROUPS):
            half = group * PIECE // HEAD_DIM
            lanes = slice(half * HEAD_DIM, (half + 1) * HEAD_DIM)
            stat = jnp.where(
                which == 0, high[:, lanes], jnp.where(which == 1, middle[:, lanes], low[:, lanes])
            )
            piece = span * GROUPS + group
            out_ref[piece, :PIECE, :] = mixed[group * PIECE : (group + 1) * PIECE]
            out_ref[piece, PIECE:, :] = stat.astype(jnp.bfloat16)


def merge_kernel(parts_ref, out_ref, turn_ref):
    me = lax.axis_index("head")
    ring, core = me // CORES, lax.rem(me, CORES)
    slots = []
    for step in range(RING):
        there = lax.rem(ring + RING - step, RING) * CORES
        slots += [there + core, there + (CORES - 1 - core)]
    rows = []
    for s in range(SPANS):
        for group in slots:
            stats = parts_ref[s * GROUPS + group, PIECE:, :].astype(jnp.float32)
            rows.append(stats[0:1] + stats[1:2] + stats[2:3])
    pad = jnp.zeros((HEAD_DIM - SPANS * GROUPS, HEAD_DIM), jnp.float32)
    turn_ref[...] = jnp.transpose(jnp.concatenate(rows + [pad], axis=0))
    begin = lax.rem(me, HEAD_DIM // PIECE) * PIECE
    mine = turn_ref[pl.ds(pl.multiple_of(begin, PIECE), PIECE), :]
    for slot, group in enumerate(slots):
        cols = [mine[:, s * GROUPS + slot : s * GROUPS + slot + 1] for s in range(SPANS)]
        highest = functools.reduce(jnp.maximum, cols)
        shares = [jnp.exp2(c - highest) for c in cols]
        total = functools.reduce(jnp.add, shares)
        mixed = jnp.zeros((PIECE, HEAD_DIM), jnp.float32)
        for s in range(SPANS):
            part = parts_ref[s * GROUPS + group, :PIECE, :].astype(jnp.float32)
            mixed = mixed + part * (shares[s] / total)
        mixed = mixed.astype(jnp.bfloat16)
        for place in range(PLACES):
            out_ref[place, :, slot * HEAD_DIM : (slot + 1) * HEAD_DIM] = mixed


def project_kernel(level_ref, rows_ref, gate_ref, *refs):
    blocks, out_ref = refs[:GROUPS], refs[GROUPS]
    acc = jnp.zeros((BLOCKS * PIECE, out_ref.shape[1]), jnp.float32)
    for pair in range(RING):
        lanes = slice(2 * pair * HEAD_DIM, 2 * (pair + 1) * HEAD_DIM)
        for head in range(HEADS_HERE):
            left = jnp.concatenate(
                [rows_ref[head * BLOCKS + b, :, lanes] for b in range(BLOCKS)], axis=0
            )
            mine = slice(head * HEAD_DIM, (head + 1) * HEAD_DIM)
            right = jnp.concatenate(
                [blocks[2 * pair][:, mine], blocks[2 * pair + 1][:, mine]], axis=1
            )
            acc = acc + lax.dot_general(
                left, right, (((1,), (1,)), ((), ())), preferred_element_type=jnp.float32
            )
    level = level_ref[lax.axis_index("span")]
    gated = (acc * gate_ref[pl.ds(level, 1), :]).astype(jnp.bfloat16)
    for block in range(BLOCKS):
        for side in range(2):
            source = block * PIECE + side * QROWS
            target = side * ROWS + block * QROWS
            out_ref[target : target + QROWS, :] = gated[source : source + QROWS]


def along_ring(x, step):
    moves = [
        (r * CORES + c, (r + step) % RING * CORES + c) for r in range(RING) for c in range(CORES)
    ]
    return lax.ppermute(x, "head", moves)


def across_cores(x):
    return lax.ppermute(x, "head", [(g, g ^ 1) for g in range(GROUPS)])


def shards(queries, keys, values, out_weight, gate_table, noise_level, span_order):
    shard = (ROWS, HEADS_HERE * HEAD_DIM)
    packed = pl.pallas_call(
        pack_kernel,
        out_shape=jax.ShapeDtypeStruct((SPANS * PLACES, QROWS + 2 * KROWS, HEAD_DIM), jnp.bfloat16),
        in_specs=[HBM] * 3,
        out_specs=VMEM,
        scratch_shapes=[pltpu.VMEM(shard, jnp.bfloat16)] * 3
        + [
            pltpu.VMEM((SPANS, 2 * KROWS, shard[1]), jnp.float32),
            pltpu.SemaphoreType.DMA((3,)),
        ],
        compiler_params=params(),
        name="pack",
    )(queries, keys, values)
    packed, weight = lax.optimization_barrier((packed, out_weight.T))
    weights = [weight] + [along_ring(weight, step) for step in range(1, RING)]
    rows = lax.all_to_all(packed, ("span", "seq"), 0, 0, tiled=True)
    parts = pl.pallas_call(
        attend_kernel,
        out_shape=jax.ShapeDtypeStruct((SPANS * GROUPS, PIECE + STATS, HEAD_DIM), jnp.bfloat16),
        in_specs=[SMEM, VMEM],
        out_specs=VMEM,
        scratch_shapes=[pltpu.VMEM((SPANS * KBLOCK, HEAD_DIM), jnp.float32)] * 2,
        compiler_params=params(),
        name="attend",
    )(span_order, rows)
    parts, weights = lax.optimization_barrier((parts, weights))
    others = [across_cores(w) for w in weights]
    parts = lax.all_to_all(parts, ("span", "head"), 0, 0, tiled=True)
    parts, others = lax.optimization_barrier((parts, others))
    blocks = [w for pair in zip(weights, others) for w in pair]
    merged = pl.pallas_call(
        merge_kernel,
        out_shape=jax.ShapeDtypeStruct((PLACES, PIECE, GROUPS * HEAD_DIM), jnp.bfloat16),
        in_specs=[VMEM],
        out_specs=VMEM,
        scratch_shapes=[pltpu.VMEM((HEAD_DIM, HEAD_DIM), jnp.float32)],
        compiler_params=params(),
        name="merge",
    )(parts)
    merged = lax.all_to_all(merged, "seq", 0, 0, tiled=True)
    return pl.pallas_call(
        project_kernel,
        out_shape=jax.ShapeDtypeStruct((BLOCKS * PIECE, out_weight.shape[1]), jnp.bfloat16),
        in_specs=[SMEM] + [VMEM] * (2 + GROUPS),
        out_specs=VMEM,
        compiler_params=params(),
        name="project",
    )(noise_level, merged, gate_table, *blocks)


def solution(mesh):
    return jax.shard_map(
        shards,
        mesh=mesh,
        in_specs=(
            P(("span", "seq"), "head"),
            P(("span", "seq"), "head"),
            P(("span", "seq"), "head"),
            P("head", "seq"),
            P(None, "seq"),
            P(),
            P(),
        ),
        out_specs=P(("span", "head"), "seq"),
        check_vma=False,
    )
```

```python
import functools
import math

import jax
import jax.numpy as jnp
from jax import lax
from jax.experimental import pallas as pl
from jax.experimental.pallas import tpu as pltpu
from jax.sharding import PartitionSpec as P

HEAD_DIM = 128
SPANS = 4
RING, CORES = 4, 2
GROUPS = 8
HEADS_HERE = 5
BLOCKS = 3
PLACES = 16
ROWS = 48
QROWS = ROWS // BLOCKS
KROWS = ROWS // SPANS
KBLOCK = PLACES * KROWS
QBLOCK = PLACES * QROWS
PIECE = QBLOCK // GROUPS
STATS = 8
HEAD = ("ring", "core")
SEQ = ("far", "side", "part")
EXP2_SCALE = math.log2(math.e) / math.sqrt(HEAD_DIM)
VMEM = pl.BlockSpec(memory_space=pltpu.VMEM)
HBM = pl.BlockSpec(memory_space=pltpu.HBM)
SMEM = pl.BlockSpec(memory_space=pltpu.SMEM)


def params(mib=24):
    return pltpu.CompilerParams(vmem_limit_bytes=mib * 2**20)


def pack_kernel(q_hbm, k_hbm, v_hbm, out_ref, q_ref, k_ref, v_ref, kv_ref, sems):
    copies = [
        pltpu.make_async_copy(source, target, sems.at[i])
        for i, (source, target) in enumerate(((q_hbm, q_ref), (k_hbm, k_ref), (v_hbm, v_ref)))
    ]
    for copy in copies:
        copy.start()
    for span in range(SPANS):
        for place in range(HEADS_HERE * BLOCKS, PLACES):
            out_ref[span * PLACES + place] = jnp.zeros(out_ref.shape[1:], out_ref.dtype)
    copies[0].wait()
    for head in range(HEADS_HERE):
        cols = slice(head * HEAD_DIM, (head + 1) * HEAD_DIM)
        for block in range(BLOCKS):
            part = q_ref[block * QROWS : (block + 1) * QROWS, cols]
            for span in range(SPANS):
                out_ref[span * PLACES + head * BLOCKS + block, :QROWS, :] = part
    copies[1].wait()
    copies[2].wait()
    key_rows = k_ref[...].astype(jnp.float32)
    value_rows = v_ref[...].astype(jnp.float32)
    for span in range(SPANS):
        kv_ref[span, :KROWS, :] = key_rows[span * KROWS : (span + 1) * KROWS]
        kv_ref[span, KROWS:, :] = value_rows[span * KROWS : (span + 1) * KROWS]
    for span in range(SPANS):
        both = kv_ref[span].astype(jnp.bfloat16)
        for head in range(HEADS_HERE):
            part = both[:, head * HEAD_DIM : (head + 1) * HEAD_DIM]
            for block in range(BLOCKS):
                out_ref[span * PLACES + head * BLOCKS + block, QROWS:, :] = part


def split_three(x):
    high = x.astype(jnp.bfloat16)
    rest = x - high.astype(jnp.float32)
    middle = rest.astype(jnp.bfloat16)
    low = (rest - middle.astype(jnp.float32)).astype(jnp.bfloat16)
    return high, middle, low


def attend_kernel(order_ref, rows_ref, out_ref, keys_ref, values_ref):
    which = lax.broadcasted_iota(jnp.int32, (STATS, HEAD_DIM), 0)
    for turn in range(SPANS):
        span = jnp.int32(0)
        for other in range(1, SPANS):
            span = span + jnp.where(order_ref[other] == turn, other, 0)
        first = span * PLACES
        for place in range(PLACES):
            both = rows_ref[first + place, QROWS:, :].astype(jnp.float32)
            target = turn * KBLOCK + place * KROWS
            keys_ref[target : target + KROWS, :] = both[:KROWS]
            values_ref[target : target + KROWS, :] = both[KROWS:]
        seen = (turn + 1) * KBLOCK
        keys = keys_ref[:seen, :].astype(jnp.bfloat16)
        values = values_ref[:seen, :].astype(jnp.bfloat16)
        own = rows_ref[pl.ds(first, PLACES), :QROWS, :].reshape(QBLOCK, HEAD_DIM)
        scores = lax.dot_general(
            own, keys, (((1,), (1,)), ((), ())), preferred_element_type=jnp.float32
        )
        scores = scores * EXP2_SCALE
        highest = jnp.max(scores, axis=1, keepdims=True)
        weights = jnp.exp2(scores - highest)
        total = jnp.sum(weights, axis=1, keepdims=True)
        mixed = jnp.dot(weights.astype(jnp.bfloat16), values, preferred_element_type=jnp.float32)
        mixed = (mixed / total).astype(jnp.bfloat16)
        logsum = highest + jnp.log2(total)
        wide = jnp.transpose(jnp.broadcast_to(logsum, (QBLOCK, HEAD_DIM)))
        high, middle, low = (t.astype(jnp.float32) for t in split_three(wide[:STATS]))
        for group in range(GROUPS):
            half = group * PIECE // HEAD_DIM
            lanes = slice(half * HEAD_DIM, (half + 1) * HEAD_DIM)
            stat = jnp.where(
                which == 0, high[:, lanes], jnp.where(which == 1, middle[:, lanes], low[:, lanes])
            )
            piece = span * GROUPS + group
            out_ref[piece, :PIECE, :] = mixed[group * PIECE : (group + 1) * PIECE]
            out_ref[piece, PIECE:, :] = stat.astype(jnp.bfloat16)


def merge_kernel(parts_ref, out_ref, turn_ref):
    ring, core = lax.axis_index("ring"), lax.axis_index("core")
    slots = []
    for step in range(RING):
        there = lax.rem(ring + step, RING) * CORES
        slots += [there + c for c in range(CORES)]
    rows = []
    for s in range(SPANS):
        for group in slots:
            stats = parts_ref[s * GROUPS + group, PIECE:, :].astype(jnp.float32)
            rows.append(stats[0:1] + stats[1:2] + stats[2:3])
    pad = jnp.zeros((HEAD_DIM - SPANS * GROUPS, HEAD_DIM), jnp.float32)
    turn_ref[...] = jnp.transpose(jnp.concatenate(rows + [pad], axis=0))
    begin = lax.rem(ring * CORES + core, HEAD_DIM // PIECE) * PIECE
    mine = turn_ref[pl.ds(pl.multiple_of(begin, PIECE), PIECE), :]
    for slot, group in enumerate(slots):
        cols = [mine[:, s * GROUPS + slot : s * GROUPS + slot + 1] for s in range(SPANS)]
        highest = functools.reduce(jnp.maximum, cols)
        shares = [jnp.exp2(c - highest) for c in cols]
        total = functools.reduce(jnp.add, shares)
        mixed = jnp.zeros((PIECE, HEAD_DIM), jnp.float32)
        for s in range(SPANS):
            part = parts_ref[s * GROUPS + group, :PIECE, :].astype(jnp.float32)
            mixed = mixed + part * (shares[s] / total)
        mixed = mixed.astype(jnp.bfloat16)
        step, half = slot // CORES, slot % CORES
        side = step % 2
        lanes = slice(0, HEAD_DIM) if step in (0, 3) else slice(HEAD_DIM, 2 * HEAD_DIM)
        for place in range(PLACES):
            if side_of(place) == side:
                out_ref[half * PLACES + place, :, lanes] = mixed


def project_kernel(rows_ref, mine_a, mine_b, theirs_a, theirs_b, out_ref):
    side = lax.axis_index("side")
    width = out_ref.shape[2]
    acc = jnp.zeros((CORES * BLOCKS * PIECE, 2 * width), jnp.float32)
    for head in range(HEADS_HERE):
        left = jnp.concatenate(
            [
                rows_ref[c * PLACES + head * BLOCKS + b]
                for c in range(CORES)
                for b in range(BLOCKS)
            ],
            axis=0,
        )
        cols = slice(head * HEAD_DIM, (head + 1) * HEAD_DIM)
        right = jnp.concatenate(
            [
                jnp.concatenate([first[:, cols], second[:, cols]], axis=1)
                for first, second in ((mine_a, mine_b), (theirs_a, theirs_b))
            ],
            axis=0,
        )
        acc = acc + lax.dot_general(
            left, right, (((1,), (1,)), ((), ())), preferred_element_type=jnp.float32
        )
    acc = acc.astype(jnp.bfloat16)
    for core in range(CORES):
        for block in range(BLOCKS):
            for half in range(2):
                source = (core * BLOCKS + block) * PIECE + half * QROWS
                target = half * ROWS + block * QROWS
                part = acc[source : source + QROWS]
                out_ref[core * 2 + side, target : target + QROWS, :] = part[:, :width]
                out_ref[core * 2 + 1 - side, target : target + QROWS, :] = part[:, width:]


def finish_kernel(level_ref, parts_ref, gate_ref, out_ref):
    level = level_ref[lax.axis_index("span")]
    total = parts_ref[0].astype(jnp.float32)
    for i in range(1, parts_ref.shape[0]):
        total = total + parts_ref[i].astype(jnp.float32)
    out_ref[...] = (total * gate_ref[pl.ds(level, 1), :]).astype(jnp.bfloat16)


def side_of(place):
    return place // 2 % 2


def near_weights(x):
    moves = [
        ((r * 4 + z) * 2 + i, ((r + i) % RING * 4 + z) * 2 + i)
        for r in range(RING)
        for z in range(4)
        for i in range(2)
    ]
    return lax.ppermute(x, ("ring", "far", "side"), moves)


def far_weights(x):
    moves = [
        ((r * 4 + z) * 2 + i, ((r + RING - 2 + i) % RING * 4 + z) * 2 + i)
        for r in range(RING)
        for z in range(4)
        for i in range(2)
    ]
    return lax.ppermute(x, ("ring", "far", "side"), moves)


def shards(queries, keys, values, out_weight, gate_table, noise_level, span_order):
    shard = (ROWS, HEADS_HERE * HEAD_DIM)
    packed = pl.pallas_call(
        pack_kernel,
        out_shape=jax.ShapeDtypeStruct((SPANS * PLACES, QROWS + 2 * KROWS, HEAD_DIM), jnp.bfloat16),
        in_specs=[HBM] * 3,
        out_specs=VMEM,
        scratch_shapes=[pltpu.VMEM(shard, jnp.bfloat16)] * 3
        + [
            pltpu.VMEM((SPANS, 2 * KROWS, shard[1]), jnp.float32),
            pltpu.SemaphoreType.DMA((3,)),
        ],
        compiler_params=params(60),
        name="pack",
    )(queries, keys, values)
    packed, weight = lax.optimization_barrier((packed, out_weight.T))
    swapped = lax.ppermute(weight, "side", [(0, 1), (1, 0)])
    mine = near_weights(weight), far_weights(weight)
    rows = lax.all_to_all(packed, ("span",) + SEQ, 0, 0, tiled=True)
    parts = pl.pallas_call(
        attend_kernel,
        out_shape=jax.ShapeDtypeStruct((SPANS * GROUPS, PIECE + STATS, HEAD_DIM), jnp.bfloat16),
        in_specs=[SMEM, VMEM],
        out_specs=VMEM,
        scratch_shapes=[pltpu.VMEM((SPANS * KBLOCK, HEAD_DIM), jnp.float32)] * 2,
        compiler_params=params(),
        name="attend",
    )(span_order, rows)
    parts, mine, swapped = lax.optimization_barrier((parts, mine, swapped))
    near = near_weights(swapped)
    parts = lax.all_to_all(parts, ("span",) + HEAD, 0, 0, tiled=True)
    merged = pl.pallas_call(
        merge_kernel,
        out_shape=jax.ShapeDtypeStruct((CORES * PLACES, PIECE, 2 * HEAD_DIM), jnp.bfloat16),
        in_specs=[VMEM],
        out_specs=VMEM,
        scratch_shapes=[pltpu.VMEM((HEAD_DIM, HEAD_DIM), jnp.float32)],
        compiler_params=params(),
        name="merge",
    )(parts)
    merged, near, swapped = lax.optimization_barrier((merged, near, swapped))
    theirs = near, far_weights(swapped)
    merged = lax.all_to_all(merged, ("core",) + SEQ, 0, 0, tiled=True)
    shape = (BLOCKS * PIECE, out_weight.shape[1])
    sums = pl.pallas_call(
        project_kernel,
        out_shape=jax.ShapeDtypeStruct((2 * CORES,) + shape, jnp.bfloat16),
        in_specs=[VMEM] * 5,
        out_specs=VMEM,
        compiler_params=params(),
        name="project",
    )(merged, *mine, *theirs)
    sums = lax.all_to_all(sums, ("core", "side"), 0, 0, tiled=True)
    return pl.pallas_call(
        finish_kernel,
        out_shape=jax.ShapeDtypeStruct(shape, jnp.bfloat16),
        in_specs=[SMEM, VMEM, VMEM],
        out_specs=VMEM,
        compiler_params=params(),
        name="finish",
    )(noise_level, sums, gate_table)


def solution(mesh):
    fine = jax.sharding.Mesh(
        mesh.devices.reshape(SPANS, RING, CORES, 4, 2, 2),
        ("span", "ring", "core", "far", "side", "part"),
    )
    return jax.shard_map(
        shards,
        mesh=fine,
        in_specs=(
            P(("span",) + SEQ, HEAD),
            P(("span",) + SEQ, HEAD),
            P(("span",) + SEQ, HEAD),
            P(HEAD, SEQ),
            P(None, SEQ),
            P(),
            P(),
        ),
        out_specs=P(("span",) + HEAD, SEQ),
        check_vma=False,
    )
```

```python
import functools
import math

import jax
import jax.numpy as jnp
from jax import lax
from jax.experimental import pallas as pl
from jax.experimental.pallas import tpu as pltpu
from jax.sharding import PartitionSpec as P

HEAD_DIM = 128
SPANS = 4
RING, CORES = 4, 2
GROUPS = 8
HEADS_HERE = 5
BLOCKS = 3
PLACES = 16
ROWS = 48
QROWS = ROWS // BLOCKS
KROWS = ROWS // SPANS
KBLOCK = PLACES * KROWS
QBLOCK = PLACES * QROWS
CHUNK = 2 * QROWS
CUT = 192
STATS = 8
HEAD = ("ring", "core")
SEQ = ("far", "side", "part")
EXP2_SCALE = math.log2(math.e) / math.sqrt(HEAD_DIM)
VMEM = pl.BlockSpec(memory_space=pltpu.VMEM)
HBM = pl.BlockSpec(memory_space=pltpu.HBM)
SMEM = pl.BlockSpec(memory_space=pltpu.SMEM)


def params(mib=24):
    return pltpu.CompilerParams(vmem_limit_bytes=mib * 2**20)


def pack_kernel(q_hbm, k_hbm, v_hbm, out_ref, q_ref, k_ref, v_ref, kv_ref, sems):
    copies = [
        pltpu.make_async_copy(source, target, sems.at[i])
        for i, (source, target) in enumerate(((q_hbm, q_ref), (k_hbm, k_ref), (v_hbm, v_ref)))
    ]
    for copy in copies:
        copy.start()
    for span in range(SPANS):
        for place in range(HEADS_HERE * BLOCKS, PLACES):
            out_ref[span * PLACES + place] = jnp.zeros(out_ref.shape[1:], out_ref.dtype)
    copies[0].wait()
    for head in range(HEADS_HERE):
        cols = slice(head * HEAD_DIM, (head + 1) * HEAD_DIM)
        for block in range(BLOCKS):
            part = q_ref[block * QROWS : (block + 1) * QROWS, cols]
            for span in range(SPANS):
                out_ref[span * PLACES + head * BLOCKS + block, :QROWS, :] = part
    copies[1].wait()
    copies[2].wait()
    key_rows = k_ref[...].astype(jnp.float32)
    value_rows = v_ref[...].astype(jnp.float32)
    for span in range(SPANS):
        kv_ref[span, :KROWS, :] = key_rows[span * KROWS : (span + 1) * KROWS]
        kv_ref[span, KROWS:, :] = value_rows[span * KROWS : (span + 1) * KROWS]
    for span in range(SPANS):
        both = kv_ref[span].astype(jnp.bfloat16)
        for head in range(HEADS_HERE):
            part = both[:, head * HEAD_DIM : (head + 1) * HEAD_DIM]
            for block in range(BLOCKS):
                out_ref[span * PLACES + head * BLOCKS + block, QROWS:, :] = part


def split_three(x):
    high = x.astype(jnp.bfloat16)
    rest = x - high.astype(jnp.float32)
    middle = rest.astype(jnp.bfloat16)
    low = (rest - middle.astype(jnp.float32)).astype(jnp.bfloat16)
    return high, middle, low


def attend_kernel(order_ref, rows_ref, out_ref, keys_ref, values_ref):
    which = lax.broadcasted_iota(jnp.int32, (STATS, HEAD_DIM), 0)
    for turn in range(SPANS):
        span = jnp.int32(0)
        for other in range(1, SPANS):
            span = span + jnp.where(order_ref[other] == turn, other, 0)
        first = span * PLACES
        for place in range(PLACES):
            both = rows_ref[first + place, QROWS:, :].astype(jnp.float32)
            target = turn * KBLOCK + place * KROWS
            keys_ref[target : target + KROWS, :] = both[:KROWS]
            values_ref[target : target + KROWS, :] = both[KROWS:]
        seen = (turn + 1) * KBLOCK
        keys = keys_ref[:seen, :].astype(jnp.bfloat16)
        values = values_ref[:seen, :].astype(jnp.bfloat16)
        own = rows_ref[pl.ds(first, PLACES), :QROWS, :].reshape(QBLOCK, HEAD_DIM)
        scores = lax.dot_general(
            own, keys, (((1,), (1,)), ((), ())), preferred_element_type=jnp.float32
        )
        scores = scores * EXP2_SCALE
        highest = jnp.max(scores, axis=1, keepdims=True)
        weights = jnp.exp2(scores - highest)
        total = jnp.sum(weights, axis=1, keepdims=True)
        mixed = jnp.dot(weights.astype(jnp.bfloat16), values, preferred_element_type=jnp.float32)
        mixed = (mixed / total).astype(jnp.bfloat16)
        logsum = highest + jnp.log2(total)
        wide = jnp.transpose(jnp.broadcast_to(logsum, (QBLOCK, HEAD_DIM)))
        terms = [t.astype(jnp.float32) for t in split_three(wide[:STATS])]
        stat = jnp.zeros((STATS, HEAD_DIM), jnp.float32)
        for half in range(2):
            lanes = slice(half * HEAD_DIM, (half + 1) * HEAD_DIM)
            for i, term in enumerate(terms):
                stat = jnp.where(which == 3 * half + i, term[:, lanes], stat)
        for core in range(CORES):
            piece = span * CORES + core
            for ring in range(RING):
                source = (ring * CORES + core) * CHUNK
                out_ref[piece, ring * CHUNK : (ring + 1) * CHUNK, :] = mixed[source : source + CHUNK]
            out_ref[piece, RING * CHUNK :, :] = stat.astype(jnp.bfloat16)


def merge_kernel(parts_ref, out_ref, turn_ref):
    core = lax.axis_index("core")
    slots = (core, CORES - 1 - core)
    rows = []
    for half in range(2):
        for slot in slots:
            for s in range(SPANS):
                stats = parts_ref[s * CORES + slot, RING * CHUNK :, :].astype(jnp.float32)
                first = 3 * half
                rows.append(stats[first : first + 1] + stats[first + 1 : first + 2] + stats[first + 2 : first + 3])
    pad = jnp.zeros((HEAD_DIM - len(rows), HEAD_DIM), jnp.float32)
    turn_ref[...] = jnp.transpose(jnp.concatenate(rows + [pad], axis=0))
    for ring in range(RING):
        half, inner = divmod(ring, HEAD_DIM // (CORES * CHUNK))
        begin = pl.multiple_of((inner * CORES + core) * CHUNK, CHUNK)
        mine = turn_ref[pl.ds(begin, CHUNK), :]
        for i, slot in enumerate(slots):
            first = (half * CORES + i) * SPANS
            cols = [mine[:, first + s : first + s + 1] for s in range(SPANS)]
            highest = functools.reduce(jnp.maximum, cols)
            shares = [jnp.exp2(c - highest) for c in cols]
            total = functools.reduce(jnp.add, shares)
            mixed = jnp.zeros((CHUNK, HEAD_DIM), jnp.float32)
            for s in range(SPANS):
                part = parts_ref[s * CORES + slot, ring * CHUNK : (ring + 1) * CHUNK, :]
                mixed = mixed + part.astype(jnp.float32) * (shares[s] / total)
            mixed = mixed.astype(jnp.bfloat16)
            lanes = slice(i * HEAD_DIM, (i + 1) * HEAD_DIM)
            for place in range(PLACES):
                side = side_of(place)
                out_ref[place, ring * QROWS : (ring + 1) * QROWS, lanes] = mixed[
                    side * QROWS : (side + 1) * QROWS
                ]


def project_kernel(rows_ref, own_ref, other_ref, *refs):
    swaps, out_ref = refs[:4], refs[4]
    side = lax.axis_index("side")
    left = [
        jnp.concatenate(
            [
                jnp.concatenate(
                    [rows_ref[head * BLOCKS + b, :, lanes] for b in range(BLOCKS)], axis=0
                )
                for head in range(HEADS_HERE)
            ],
            axis=1,
        )
        for lanes in (slice(0, HEAD_DIM), slice(HEAD_DIM, 2 * HEAD_DIM))
    ]
    own, other = (jnp.concatenate([a[...], b[...]], axis=0) for a, b in (swaps[:2], swaps[2:]))
    for weights, target in (((own_ref[...], other_ref[...]), side), ((own, other), 1 - side)):
        sums = [
            lax.dot_general(x, w, (((1,), (1,)), ((), ())), preferred_element_type=jnp.float32)
            for x, w in zip(left, weights)
        ]
        total = (sums[0] + sums[1]).astype(jnp.bfloat16)
        for ring in range(RING):
            for block in range(BLOCKS):
                source = (block * RING + ring) * QROWS
                out_ref[ring * 2 + target, block * QROWS : (block + 1) * QROWS, :] = total[
                    source : source + QROWS
                ]


def finish_kernel(level_ref, parts_ref, gate_ref, out_ref):
    level = level_ref[lax.axis_index("span")]
    gate = gate_ref[pl.ds(level, 1), :]
    for side in range(2):
        total = parts_ref[side].astype(jnp.float32)
        for ring in range(1, RING):
            total = total + parts_ref[ring * 2 + side].astype(jnp.float32)
        out_ref[side * ROWS : (side + 1) * ROWS, :] = (total * gate).astype(jnp.bfloat16)


def side_of(place):
    return place // 2 % 2


def swap_sides(x):
    return lax.ppermute(x, "side", [(0, 1), (1, 0)])


def swap_cores(x):
    return lax.ppermute(x, "core", [(0, 1), (1, 0)])


def shards(queries, keys, values, out_weight, gate_table, noise_level, span_order):
    shard = (ROWS, HEADS_HERE * HEAD_DIM)
    packed = pl.pallas_call(
        pack_kernel,
        out_shape=jax.ShapeDtypeStruct((SPANS * PLACES, QROWS + 2 * KROWS, HEAD_DIM), jnp.bfloat16),
        in_specs=[HBM] * 3,
        out_specs=VMEM,
        scratch_shapes=[pltpu.VMEM(shard, jnp.bfloat16)] * 3
        + [
            pltpu.VMEM((SPANS, 2 * KROWS, shard[1]), jnp.float32),
            pltpu.SemaphoreType.DMA((3,)),
        ],
        compiler_params=params(60),
        name="pack",
    )(queries, keys, values)
    packed, weight = lax.optimization_barrier((packed, out_weight.T))
    other = swap_cores(weight)
    first = swap_sides(weight[:CUT])
    rows = lax.all_to_all(packed, ("span",) + SEQ, 0, 0, tiled=True)
    parts = pl.pallas_call(
        attend_kernel,
        out_shape=jax.ShapeDtypeStruct((SPANS * CORES, RING * CHUNK + STATS, HEAD_DIM), jnp.bfloat16),
        in_specs=[SMEM, VMEM],
        out_specs=VMEM,
        scratch_shapes=[pltpu.VMEM((SPANS * KBLOCK, HEAD_DIM), jnp.float32)] * 2,
        compiler_params=params(),
        name="attend",
    )(span_order, rows)
    parts, first, other = lax.optimization_barrier((parts, first, other))
    second = swap_sides(weight[CUT:])
    parts = lax.all_to_all(parts, ("span", "core"), 0, 0, tiled=True)
    parts, second = lax.optimization_barrier((parts, second))
    merged = pl.pallas_call(
        merge_kernel,
        out_shape=jax.ShapeDtypeStruct((PLACES, RING * QROWS, CORES * HEAD_DIM), jnp.bfloat16),
        in_specs=[VMEM],
        out_specs=VMEM,
        scratch_shapes=[pltpu.VMEM((HEAD_DIM, HEAD_DIM), jnp.float32)],
        compiler_params=params(),
        name="merge",
    )(parts)
    merged, first, second = lax.optimization_barrier((merged, first, second))
    first_other, second_other = swap_cores(first), swap_cores(second)
    merged = lax.all_to_all(merged, SEQ, 0, 0, tiled=True)
    sums = pl.pallas_call(
        project_kernel,
        out_shape=jax.ShapeDtypeStruct((RING * 2, ROWS, out_weight.shape[1]), jnp.bfloat16),
        in_specs=[VMEM] * 7,
        out_specs=VMEM,
        compiler_params=params(),
        name="project",
    )(merged, weight, other, first, second, first_other, second_other)
    sums = lax.all_to_all(sums, ("ring", "side"), 0, 0, tiled=True)
    return pl.pallas_call(
        finish_kernel,
        out_shape=jax.ShapeDtypeStruct((2 * ROWS, out_weight.shape[1]), jnp.bfloat16),
        in_specs=[SMEM, VMEM, VMEM],
        out_specs=VMEM,
        compiler_params=params(),
        name="finish",
    )(noise_level, sums, gate_table)


def solution(mesh):
    fine = jax.sharding.Mesh(
        mesh.devices.reshape(SPANS, RING, CORES, 4, 2, 2),
        ("span", "ring", "core", "far", "side", "part"),
    )
    return jax.shard_map(
        shards,
        mesh=fine,
        in_specs=(
            P(("span",) + SEQ, HEAD),
            P(("span",) + SEQ, HEAD),
            P(("span",) + SEQ, HEAD),
            P(HEAD, SEQ),
            P(None, SEQ),
            P(),
            P(),
        ),
        out_specs=P(("span",) + HEAD, SEQ),
        check_vma=False,
    )
```

```python
import functools
import math

import jax
import jax.numpy as jnp
from jax import lax
from jax.experimental import pallas as pl
from jax.experimental.pallas import tpu as pltpu
from jax.sharding import PartitionSpec as P

HEAD_DIM = 128
SPANS = 4
RING, CORES = 4, 2
GROUPS = 8
HEADS_HERE = 5
BLOCKS = 3
PLACES = 16
ROWS = 48
QROWS = ROWS // BLOCKS
KROWS = ROWS // SPANS
KBLOCK = PLACES * KROWS
QBLOCK = PLACES * QROWS
CHUNK = 2 * QROWS
CUT = 176
STATS = 8
HEAD = ("ring", "core")
SEQ = ("far", "side", "part")
EXP2_SCALE = math.log2(math.e) / math.sqrt(HEAD_DIM)
VMEM = pl.BlockSpec(memory_space=pltpu.VMEM)
HBM = pl.BlockSpec(memory_space=pltpu.HBM)


def params(mib=24):
    return pltpu.CompilerParams(vmem_limit_bytes=mib * 2**20)


def pack_kernel(q_hbm, k_hbm, v_hbm, out_ref, q_ref, k_ref, v_ref, kv_ref, sems):
    copies = [
        pltpu.make_async_copy(source, target, sems.at[i])
        for i, (source, target) in enumerate(((q_hbm, q_ref), (k_hbm, k_ref), (v_hbm, v_ref)))
    ]
    for copy in copies:
        copy.start()
    for span in range(SPANS):
        for place in range(HEADS_HERE * BLOCKS, PLACES):
            out_ref[span * PLACES + place] = jnp.zeros(out_ref.shape[1:], out_ref.dtype)
    copies[0].wait()
    for head in range(HEADS_HERE):
        cols = slice(head * HEAD_DIM, (head + 1) * HEAD_DIM)
        for block in range(BLOCKS):
            part = q_ref[block * QROWS : (block + 1) * QROWS, cols]
            for span in range(SPANS):
                out_ref[span * PLACES + head * BLOCKS + block, :QROWS, :] = part
    copies[1].wait()
    copies[2].wait()
    key_rows = k_ref[...].astype(jnp.float32)
    value_rows = v_ref[...].astype(jnp.float32)
    for span in range(SPANS):
        kv_ref[span, :KROWS, :] = key_rows[span * KROWS : (span + 1) * KROWS]
        kv_ref[span, KROWS:, :] = value_rows[span * KROWS : (span + 1) * KROWS]
    for span in range(SPANS):
        both = kv_ref[span].astype(jnp.bfloat16)
        for head in range(HEADS_HERE):
            part = both[:, head * HEAD_DIM : (head + 1) * HEAD_DIM]
            for block in range(BLOCKS):
                out_ref[span * PLACES + head * BLOCKS + block, QROWS:, :] = part


def split_three(x):
    high = x.astype(jnp.bfloat16)
    rest = x - high.astype(jnp.float32)
    middle = rest.astype(jnp.bfloat16)
    low = (rest - middle.astype(jnp.float32)).astype(jnp.bfloat16)
    return high, middle, low


def attend_kernel(order_ref, rows_ref, out_ref, keys_ref, values_ref):
    line = order_ref[...]
    order = [line[0, i] for i in range(SPANS)]
    spans = []
    for turn in range(SPANS):
        span = jnp.int32(0)
        for other in range(1, SPANS):
            span = span + jnp.where(order[other] == turn, other, 0)
        spans.append(span)
        for place in range(PLACES):
            both = rows_ref[span * PLACES + place, QROWS:, :].astype(jnp.float32)
            target = turn * KBLOCK + place * KROWS
            keys_ref[target : target + KROWS, :] = both[:KROWS]
            values_ref[target : target + KROWS, :] = both[KROWS:]
    keys = keys_ref[...].astype(jnp.bfloat16)
    values = values_ref[...].astype(jnp.bfloat16)
    state = []
    for turn, span in enumerate(spans):
        seen = (turn + 1) * KBLOCK
        own = rows_ref[pl.ds(span * PLACES, PLACES), :QROWS, :].reshape(QBLOCK, HEAD_DIM)
        scores = lax.dot_general(
            keys[:seen], own, (((1,), (1,)), ((), ())), preferred_element_type=jnp.float32
        )
        state.append(scores)
    soft = []
    for scores in state:
        highest = jnp.max(scores, axis=0, keepdims=True) * EXP2_SCALE
        weights = jnp.exp2(scores * EXP2_SCALE - highest)
        total = jnp.sum(weights, axis=0, keepdims=True)
        soft.append((highest, weights.astype(jnp.bfloat16), total))
    for turn, span in enumerate(spans):
        seen = (turn + 1) * KBLOCK
        highest, weights, total = soft[turn]
        mixed = lax.dot_general(
            weights, values[:seen], (((0,), (0,)), ((), ())), preferred_element_type=jnp.float32
        )
        mixed = (mixed * jnp.transpose(jnp.broadcast_to(1.0 / total, (HEAD_DIM, QBLOCK)))).astype(jnp.bfloat16)
        terms = [t.astype(jnp.float32) for t in split_three(highest + jnp.log2(total))]
        stat = [t[:, half * HEAD_DIM : (half + 1) * HEAD_DIM] for half in range(2) for t in terms]
        stat = jnp.concatenate(
            stat + [jnp.zeros((STATS - len(stat), HEAD_DIM), jnp.float32)], axis=0
        )
        for core in range(CORES):
            for ring in range(RING):
                source = (ring * CORES + core) * CHUNK
                out_ref[span * CORES + core, ring * CHUNK : (ring + 1) * CHUNK, :] = mixed[
                    source : source + CHUNK
                ]
            out_ref[span * CORES + core, RING * CHUNK :, :] = stat.astype(jnp.bfloat16)


def merge_kernel(parts_ref, out_ref, turn_ref):
    core = lax.axis_index("core")
    slots = (core, CORES - 1 - core)
    rows = []
    for half in range(2):
        for slot in slots:
            for s in range(SPANS):
                stats = parts_ref[s * CORES + slot, RING * CHUNK :, :].astype(jnp.float32)
                first = 3 * half
                rows.append(stats[first : first + 1] + stats[first + 1 : first + 2] + stats[first + 2 : first + 3])
    pad = jnp.zeros((HEAD_DIM - len(rows), HEAD_DIM), jnp.float32)
    turn_ref[...] = jnp.transpose(jnp.concatenate(rows + [pad], axis=0))
    for ring in range(RING):
        half, inner = divmod(ring, HEAD_DIM // (CORES * CHUNK))
        begin = pl.multiple_of((inner * CORES + core) * CHUNK, CHUNK)
        mine = turn_ref[pl.ds(begin, CHUNK), :]
        for i, slot in enumerate(slots):
            first = (half * CORES + i) * SPANS
            cols = [mine[:, first + s : first + s + 1] for s in range(SPANS)]
            highest = functools.reduce(jnp.maximum, cols)
            shares = [jnp.exp2(c - highest) for c in cols]
            total = functools.reduce(jnp.add, shares)
            mixed = jnp.zeros((CHUNK, HEAD_DIM), jnp.float32)
            for s in range(SPANS):
                part = parts_ref[s * CORES + slot, ring * CHUNK : (ring + 1) * CHUNK, :]
                mixed = mixed + part.astype(jnp.float32) * (shares[s] / total)
            mixed = mixed.astype(jnp.bfloat16)
            lanes = slice(i * HEAD_DIM, (i + 1) * HEAD_DIM)
            for place in range(PLACES):
                side = side_of(place)
                out_ref[place, ring * QROWS : (ring + 1) * QROWS, lanes] = mixed[
                    side * QROWS : (side + 1) * QROWS
                ]


def project_kernel(rows_ref, own_ref, other_ref, *refs):
    swaps, out_ref = refs[:4], refs[4]
    side = lax.axis_index("side")
    left = [
        jnp.concatenate(
            [
                jnp.concatenate(
                    [rows_ref[head * BLOCKS + b, :, lanes] for b in range(BLOCKS)], axis=0
                )
                for head in range(HEADS_HERE)
            ],
            axis=1,
        )
        for lanes in (slice(0, HEAD_DIM), slice(HEAD_DIM, 2 * HEAD_DIM))
    ]
    own, other = (jnp.concatenate([a[...], b[...]], axis=0) for a, b in (swaps[:2], swaps[2:]))
    for weights, target in (((own_ref[...], other_ref[...]), side), ((own, other), 1 - side)):
        sums = [
            lax.dot_general(x, w, (((1,), (1,)), ((), ())), preferred_element_type=jnp.float32)
            for x, w in zip(left, weights)
        ]
        total = (sums[0] + sums[1]).astype(jnp.bfloat16)
        for ring in range(RING):
            for block in range(BLOCKS):
                source = (block * RING + ring) * QROWS
                out_ref[ring * 2 + target, block * QROWS : (block + 1) * QROWS, :] = total[
                    source : source + QROWS
                ]


def finish_kernel(parts_ref, gate_ref, out_ref):
    for side in range(2):
        total = parts_ref[side].astype(jnp.float32)
        for ring in range(1, RING):
            total = total + parts_ref[ring * 2 + side].astype(jnp.float32)
        out_ref[side * ROWS : (side + 1) * ROWS, :] = (total * gate_ref[...]).astype(jnp.bfloat16)


def side_of(place):
    return place // 2 % 2


def swap_sides(x):
    return lax.ppermute(x, "side", [(0, 1), (1, 0)])


def swap_cores(x):
    return lax.ppermute(x, "core", [(0, 1), (1, 0)])


def shards(queries, keys, values, out_weight, gate_table, noise_level, span_order):
    shard = (ROWS, HEADS_HERE * HEAD_DIM)
    packed = pl.pallas_call(
        pack_kernel,
        out_shape=jax.ShapeDtypeStruct((SPANS * PLACES, QROWS + 2 * KROWS, HEAD_DIM), jnp.bfloat16),
        in_specs=[HBM] * 3,
        out_specs=VMEM,
        scratch_shapes=[pltpu.VMEM(shard, jnp.bfloat16)] * 3
        + [
            pltpu.VMEM((SPANS, 2 * KROWS, shard[1]), jnp.float32),
            pltpu.SemaphoreType.DMA((3,)),
        ],
        compiler_params=params(60),
        name="pack",
    )(queries, keys, values)
    level = lax.dynamic_index_in_dim(noise_level, lax.axis_index("span"), 0, keepdims=False)
    gate_row = lax.dynamic_slice_in_dim(gate_table, level, 1, 0)
    packed, weight = lax.optimization_barrier((packed, out_weight.T))
    first = swap_sides(weight[:CUT])
    rows = lax.all_to_all(packed, ("span",) + SEQ, 0, 0, tiled=True)
    parts = pl.pallas_call(
        attend_kernel,
        out_shape=jax.ShapeDtypeStruct((SPANS * CORES, RING * CHUNK + STATS, HEAD_DIM), jnp.bfloat16),
        in_specs=[VMEM, VMEM],
        out_specs=VMEM,
        scratch_shapes=[pltpu.VMEM((SPANS * KBLOCK, HEAD_DIM), jnp.float32)] * 2,
        compiler_params=params(),
        name="attend",
    )(span_order.reshape(1, SPANS), rows)
    parts, first, gate_row = lax.optimization_barrier((parts, first, gate_row))
    second = swap_sides(weight[CUT:])
    parts = lax.all_to_all(parts, ("span", "core"), 0, 0, tiled=True)
    parts, second = lax.optimization_barrier((parts, second))
    merged = pl.pallas_call(
        merge_kernel,
        out_shape=jax.ShapeDtypeStruct((PLACES, RING * QROWS, CORES * HEAD_DIM), jnp.bfloat16),
        in_specs=[VMEM],
        out_specs=VMEM,
        scratch_shapes=[pltpu.VMEM((HEAD_DIM, HEAD_DIM), jnp.float32)],
        compiler_params=params(),
        name="merge",
    )(parts)
    merged, weight, first, second = lax.optimization_barrier((merged, weight, first, second))
    other, first_other, second_other = swap_cores(weight), swap_cores(first), swap_cores(second)
    merged = lax.all_to_all(merged, SEQ, 0, 0, tiled=True)
    sums = pl.pallas_call(
        project_kernel,
        out_shape=jax.ShapeDtypeStruct((RING * 2, ROWS, out_weight.shape[1]), jnp.bfloat16),
        in_specs=[VMEM] * 7,
        out_specs=VMEM,
        compiler_params=params(),
        name="project",
    )(merged, weight, other, first, second, first_other, second_other)
    sums = lax.all_to_all(sums, ("ring", "side"), 0, 0, tiled=True)
    return pl.pallas_call(
        finish_kernel,
        out_shape=jax.ShapeDtypeStruct((2 * ROWS, out_weight.shape[1]), jnp.bfloat16),
        in_specs=[VMEM, VMEM],
        out_specs=VMEM,
        compiler_params=params(),
        name="finish",
    )(sums, gate_row)


def solution(mesh):
    fine = jax.sharding.Mesh(
        mesh.devices.reshape(SPANS, RING, CORES, 4, 2, 2),
        ("span", "ring", "core", "far", "side", "part"),
    )
    return jax.shard_map(
        shards,
        mesh=fine,
        in_specs=(
            P(("span",) + SEQ, HEAD),
            P(("span",) + SEQ, HEAD),
            P(("span",) + SEQ, HEAD),
            P(HEAD, SEQ),
            P(None, SEQ),
            P(),
            P(),
        ),
        out_specs=P(("span",) + HEAD, SEQ),
        check_vma=False,
    )
```

```python
import functools
import math

import jax
import jax.numpy as jnp
from jax import lax
from jax.experimental import pallas as pl
from jax.experimental.pallas import tpu as pltpu
from jax.sharding import PartitionSpec as P

HEAD_DIM = 128
SPANS = 4
RING, CORES = 4, 2
GROUPS = 8
HEADS_HERE = 5
BLOCKS = 3
PLACES = 16
ROWS = 48
QROWS = ROWS // BLOCKS
KROWS = ROWS // SPANS
KBLOCK = PLACES * KROWS
QBLOCK = PLACES * QROWS
CHUNK = 2 * QROWS
STATS = 8
HEAD = ("ring", "core")
SEQ = ("far", "side", "part")
EXP2_SCALE = math.log2(math.e) / math.sqrt(HEAD_DIM)
VMEM = pl.BlockSpec(memory_space=pltpu.VMEM)
HBM = pl.BlockSpec(memory_space=pltpu.HBM)


def params(mib=24):
    return pltpu.CompilerParams(vmem_limit_bytes=mib * 2**20)


def spot(place):
    return place % 2 * (PLACES // 2) + place // 2


def pack_kernel(q_hbm, k_hbm, v_hbm, out_ref, q_ref, k_ref, v_ref, kv_ref, sems):
    copies = [
        pltpu.make_async_copy(source, target, sems.at[i])
        for i, (source, target) in enumerate(((q_hbm, q_ref), (k_hbm, k_ref), (v_hbm, v_ref)))
    ]
    for copy in copies:
        copy.start()
    for span in range(SPANS):
        for place in range(HEADS_HERE * BLOCKS, PLACES):
            out_ref[span * PLACES + spot(place)] = jnp.zeros(out_ref.shape[1:], out_ref.dtype)
    copies[0].wait()
    for head in range(HEADS_HERE):
        cols = slice(head * HEAD_DIM, (head + 1) * HEAD_DIM)
        for block in range(BLOCKS):
            part = q_ref[block * QROWS : (block + 1) * QROWS, cols]
            for span in range(SPANS):
                out_ref[span * PLACES + spot(head * BLOCKS + block), :QROWS, :] = part
    copies[1].wait()
    copies[2].wait()
    key_rows = k_ref[...].astype(jnp.float32)
    value_rows = v_ref[...].astype(jnp.float32)
    for span in range(SPANS):
        kv_ref[span, :KROWS, :] = key_rows[span * KROWS : (span + 1) * KROWS]
        kv_ref[span, KROWS:, :] = value_rows[span * KROWS : (span + 1) * KROWS]
    for span in range(SPANS):
        both = kv_ref[span].astype(jnp.bfloat16)
        for head in range(HEADS_HERE):
            part = both[:, head * HEAD_DIM : (head + 1) * HEAD_DIM]
            for block in range(BLOCKS):
                out_ref[span * PLACES + spot(head * BLOCKS + block), QROWS:, :] = part


def split_three(x):
    high = x.astype(jnp.bfloat16)
    rest = x - high.astype(jnp.float32)
    middle = rest.astype(jnp.bfloat16)
    low = (rest - middle.astype(jnp.float32)).astype(jnp.bfloat16)
    return high, middle, low


def attend_kernel(order_ref, rows_ref, out_ref, keys_ref, values_ref):
    line = order_ref[...]
    order = [line[0, i] for i in range(SPANS)]
    spans = []
    for turn in range(SPANS):
        span = jnp.int32(0)
        for other in range(1, SPANS):
            span = span + jnp.where(order[other] == turn, other, 0)
        spans.append(span)
        for place in range(PLACES):
            both = rows_ref[span * PLACES + place, QROWS:, :].astype(jnp.float32)
            target = turn * KBLOCK + place * KROWS
            keys_ref[target : target + KROWS, :] = both[:KROWS]
            values_ref[target : target + KROWS, :] = both[KROWS:]
    keys = keys_ref[...].astype(jnp.bfloat16)
    values = values_ref[...].astype(jnp.bfloat16)
    state = []
    for turn, span in enumerate(spans):
        seen = (turn + 1) * KBLOCK
        own = jnp.concatenate(
            [rows_ref[span * PLACES + spot(place), :QROWS, :] for place in range(PLACES)], axis=0
        )
        scores = lax.dot_general(
            keys[:seen], own, (((1,), (1,)), ((), ())), preferred_element_type=jnp.float32
        )
        state.append(scores)
    soft = []
    for scores in state:
        highest = jnp.max(scores, axis=0, keepdims=True) * EXP2_SCALE
        weights = jnp.exp2(scores * EXP2_SCALE - highest)
        total = jnp.sum(weights, axis=0, keepdims=True)
        soft.append((highest, weights.astype(jnp.bfloat16), total))
    for turn, span in enumerate(spans):
        seen = (turn + 1) * KBLOCK
        highest, weights, total = soft[turn]
        mixed = lax.dot_general(
            weights, values[:seen], (((0,), (0,)), ((), ())), preferred_element_type=jnp.float32
        )
        mixed = (mixed * jnp.transpose(jnp.broadcast_to(1.0 / total, (HEAD_DIM, QBLOCK)))).astype(jnp.bfloat16)
        terms = [t.astype(jnp.float32) for t in split_three(highest + jnp.log2(total))]
        stat = [t[:, half * HEAD_DIM : (half + 1) * HEAD_DIM] for half in range(2) for t in terms]
        stat = jnp.concatenate(
            stat + [jnp.zeros((STATS - len(stat), HEAD_DIM), jnp.float32)], axis=0
        )
        for core in range(CORES):
            for ring in range(RING):
                source = (ring * CORES + core) * CHUNK
                out_ref[span * CORES + core, ring * CHUNK : (ring + 1) * CHUNK, :] = mixed[
                    source : source + CHUNK
                ]
            out_ref[span * CORES + core, RING * CHUNK :, :] = stat.astype(jnp.bfloat16)


def merge_kernel(parts_ref, out_ref, turn_ref):
    core = lax.axis_index("core")
    slots = (core, CORES - 1 - core)
    rows = []
    for half in range(2):
        for slot in slots:
            for s in range(SPANS):
                stats = parts_ref[s * CORES + slot, RING * CHUNK :, :].astype(jnp.float32)
                first = 3 * half
                rows.append(stats[first : first + 1] + stats[first + 1 : first + 2] + stats[first + 2 : first + 3])
    pad = jnp.zeros((HEAD_DIM - len(rows), HEAD_DIM), jnp.float32)
    turn_ref[...] = jnp.transpose(jnp.concatenate(rows + [pad], axis=0))
    for ring in range(RING):
        half, inner = divmod(ring, HEAD_DIM // (CORES * CHUNK))
        begin = pl.multiple_of((inner * CORES + core) * CHUNK, CHUNK)
        mine = turn_ref[pl.ds(begin, CHUNK), :]
        for i, slot in enumerate(slots):
            first = (half * CORES + i) * SPANS
            cols = [mine[:, first + s : first + s + 1] for s in range(SPANS)]
            highest = functools.reduce(jnp.maximum, cols)
            shares = [jnp.exp2(c - highest) for c in cols]
            total = functools.reduce(jnp.add, shares)
            mixed = jnp.zeros((CHUNK, HEAD_DIM), jnp.float32)
            for s in range(SPANS):
                part = parts_ref[s * CORES + slot, ring * CHUNK : (ring + 1) * CHUNK, :]
                mixed = mixed + part.astype(jnp.float32) * (shares[s] / total)
            mixed = mixed.astype(jnp.bfloat16)
            lanes = slice(i * HEAD_DIM, (i + 1) * HEAD_DIM)
            for place in range(PLACES):
                side = side_of(place)
                out_ref[place, ring * QROWS : (ring + 1) * QROWS, lanes] = mixed[
                    side * QROWS : (side + 1) * QROWS
                ]


def project_kernel(rows_ref, own_ref, other_ref, theirs_ref, theirs_other_ref, out_ref):
    side = lax.axis_index("side")
    left = [
        jnp.concatenate(
            [
                jnp.concatenate(
                    [rows_ref[head * BLOCKS + b, :, lanes] for b in range(BLOCKS)], axis=0
                )
                for head in range(HEADS_HERE)
            ],
            axis=1,
        )
        for lanes in (slice(0, HEAD_DIM), slice(HEAD_DIM, 2 * HEAD_DIM))
    ]
    for weights, target in (
        ((own_ref, other_ref), side),
        ((theirs_ref, theirs_other_ref), 1 - side),
    ):
        sums = [
            lax.dot_general(x, w[...], (((1,), (1,)), ((), ())), preferred_element_type=jnp.float32)
            for x, w in zip(left, weights)
        ]
        total = (sums[0] + sums[1]).astype(jnp.bfloat16)
        for ring in range(RING):
            for block in range(BLOCKS):
                source = (block * RING + ring) * QROWS
                out_ref[ring * 2 + target, block * QROWS : (block + 1) * QROWS, :] = total[
                    source : source + QROWS
                ]


def finish_kernel(parts_ref, gate_ref, out_ref):
    for side in range(2):
        total = parts_ref[side].astype(jnp.float32)
        for ring in range(1, RING):
            total = total + parts_ref[ring * 2 + side].astype(jnp.float32)
        out_ref[side * ROWS : (side + 1) * ROWS, :] = (total * gate_ref[...]).astype(jnp.bfloat16)


def side_of(place):
    return place // 2 % 2


def swap_sides(x):
    return lax.ppermute(x, "side", [(0, 1), (1, 0)])


def swap_cores(x):
    return lax.ppermute(x, "core", [(0, 1), (1, 0)])


def shards(queries, keys, values, out_weight, gate_table, noise_level, span_order):
    shard = (ROWS, HEADS_HERE * HEAD_DIM)
    packed = pl.pallas_call(
        pack_kernel,
        out_shape=jax.ShapeDtypeStruct((SPANS * PLACES, QROWS + 2 * KROWS, HEAD_DIM), jnp.bfloat16),
        in_specs=[HBM] * 3,
        out_specs=VMEM,
        scratch_shapes=[pltpu.VMEM(shard, jnp.bfloat16)] * 3
        + [
            pltpu.VMEM((SPANS, 2 * KROWS, shard[1]), jnp.float32),
            pltpu.SemaphoreType.DMA((3,)),
        ],
        compiler_params=params(60),
        name="pack",
    )(queries, keys, values)
    level = lax.dynamic_index_in_dim(noise_level, lax.axis_index("span"), 0, keepdims=False)
    gate_row = lax.dynamic_slice_in_dim(gate_table, level, 1, 0)
    packed, weight = lax.optimization_barrier((packed, out_weight.T))
    theirs, other = swap_sides(weight), swap_cores(weight)
    theirs_other = swap_cores(theirs)
    rows = lax.all_to_all(packed, ("span", "part", "far", "side"), 0, 0, tiled=True)
    parts = pl.pallas_call(
        attend_kernel,
        out_shape=jax.ShapeDtypeStruct((SPANS * CORES, RING * CHUNK + STATS, HEAD_DIM), jnp.bfloat16),
        in_specs=[VMEM, VMEM],
        out_specs=VMEM,
        scratch_shapes=[pltpu.VMEM((SPANS * KBLOCK, HEAD_DIM), jnp.float32)] * 2,
        compiler_params=params(),
        name="attend",
    )(span_order.reshape(1, SPANS), rows)
    parts, other, gate_row = lax.optimization_barrier((parts, other, gate_row))
    parts = lax.all_to_all(parts, ("span", "core"), 0, 0, tiled=True)
    parts, theirs, theirs_other = lax.optimization_barrier((parts, theirs, theirs_other))
    merged = pl.pallas_call(
        merge_kernel,
        out_shape=jax.ShapeDtypeStruct((PLACES, RING * QROWS, CORES * HEAD_DIM), jnp.bfloat16),
        in_specs=[VMEM],
        out_specs=VMEM,
        scratch_shapes=[pltpu.VMEM((HEAD_DIM, HEAD_DIM), jnp.float32)],
        compiler_params=params(),
        name="merge",
    )(parts)
    merged = lax.all_to_all(merged, SEQ, 0, 0, tiled=True)
    sums = pl.pallas_call(
        project_kernel,
        out_shape=jax.ShapeDtypeStruct((RING * 2, ROWS, out_weight.shape[1]), jnp.bfloat16),
        in_specs=[VMEM] * 5,
        out_specs=VMEM,
        compiler_params=params(),
        name="project",
    )(merged, weight, other, theirs, theirs_other)
    sums = lax.all_to_all(sums, ("ring", "side"), 0, 0, tiled=True)
    return pl.pallas_call(
        finish_kernel,
        out_shape=jax.ShapeDtypeStruct((2 * ROWS, out_weight.shape[1]), jnp.bfloat16),
        in_specs=[VMEM, VMEM],
        out_specs=VMEM,
        compiler_params=params(),
        name="finish",
    )(sums, gate_row)


def solution(mesh):
    fine = jax.sharding.Mesh(
        mesh.devices.reshape(SPANS, RING, CORES, 4, 2, 2),
        ("span", "ring", "core", "far", "side", "part"),
    )
    return jax.shard_map(
        shards,
        mesh=fine,
        in_specs=(
            P(("span",) + SEQ, HEAD),
            P(("span",) + SEQ, HEAD),
            P(("span",) + SEQ, HEAD),
            P(HEAD, SEQ),
            P(None, SEQ),
            P(),
            P(),
        ),
        out_specs=P(("span",) + HEAD, SEQ),
        check_vma=False,
    )
```

```python
import functools
import math

import jax
import jax.numpy as jnp
from jax import lax
from jax.experimental import pallas as pl
from jax.experimental.pallas import tpu as pltpu
from jax.sharding import PartitionSpec as P

HEAD_DIM = 128
SPANS = 4
RING, CORES = 4, 2
GROUPS = 8
HEADS_HERE = 5
BLOCKS = 3
PLACES = 16
ROWS = 48
QROWS = ROWS // BLOCKS
KROWS = ROWS // SPANS
KBLOCK = PLACES * KROWS
QBLOCK = PLACES * QROWS
CHUNK = 2 * QROWS
STATS = 8
HEAD = ("ring", "core")
SEQ = ("far", "side", "part")
EXP2_SCALE = math.log2(math.e) / math.sqrt(HEAD_DIM)
VMEM = pl.BlockSpec(memory_space=pltpu.VMEM)
HBM = pl.BlockSpec(memory_space=pltpu.HBM)


def params(mib=24):
    return pltpu.CompilerParams(vmem_limit_bytes=mib * 2**20)


def spot(place):
    return place % 2 * (PLACES // 2) + place // 2


def pack_kernel(q_hbm, k_hbm, v_hbm, out_ref, q_ref, k_ref, v_ref, kv_ref, sems):
    copies = [
        pltpu.make_async_copy(source, target, sems.at[i])
        for i, (source, target) in enumerate(((q_hbm, q_ref), (k_hbm, k_ref), (v_hbm, v_ref)))
    ]
    for copy in copies:
        copy.start()
    for span in range(SPANS):
        for place in range(HEADS_HERE * BLOCKS, PLACES):
            out_ref[span * PLACES + spot(place)] = jnp.zeros(out_ref.shape[1:], out_ref.dtype)
    copies[0].wait()
    for head in range(HEADS_HERE):
        cols = slice(head * HEAD_DIM, (head + 1) * HEAD_DIM)
        for block in range(BLOCKS):
            part = q_ref[block * QROWS : (block + 1) * QROWS, cols]
            for span in range(SPANS):
                out_ref[span * PLACES + spot(head * BLOCKS + block), :QROWS, :] = part
    copies[1].wait()
    copies[2].wait()
    key_rows = k_ref[...].astype(jnp.float32)
    value_rows = v_ref[...].astype(jnp.float32)
    for span in range(SPANS):
        kv_ref[span, :KROWS, :] = key_rows[span * KROWS : (span + 1) * KROWS]
        kv_ref[span, KROWS:, :] = value_rows[span * KROWS : (span + 1) * KROWS]
    for span in range(SPANS):
        both = kv_ref[span].astype(jnp.bfloat16)
        for head in range(HEADS_HERE):
            part = both[:, head * HEAD_DIM : (head + 1) * HEAD_DIM]
            for block in range(BLOCKS):
                out_ref[span * PLACES + spot(head * BLOCKS + block), QROWS:, :] = part


def split_three(x):
    high = x.astype(jnp.bfloat16)
    rest = x - high.astype(jnp.float32)
    middle = rest.astype(jnp.bfloat16)
    low = (rest - middle.astype(jnp.float32)).astype(jnp.bfloat16)
    return high, middle, low


def attend_kernel(order_ref, rows_ref, out_ref, keys_ref, values_ref):
    line = order_ref[...]
    order = [line[0, i] for i in range(SPANS)]
    spans = []
    for turn in range(SPANS):
        span = jnp.int32(0)
        for other in range(1, SPANS):
            span = span + jnp.where(order[other] == turn, other, 0)
        span = jnp.minimum(span, SPANS - 1)
        spans.append(span)
        for place in range(PLACES):
            both = rows_ref[span * PLACES + place, QROWS:, :].astype(jnp.float32)
            target = turn * KBLOCK + place * KROWS
            keys_ref[target : target + KROWS, :] = both[:KROWS]
            values_ref[target : target + KROWS, :] = both[KROWS:]
    keys = keys_ref[...].astype(jnp.bfloat16)
    values = values_ref[...].astype(jnp.bfloat16)
    state = []
    for turn, span in enumerate(spans):
        seen = (turn + 1) * KBLOCK
        own = jnp.concatenate(
            [rows_ref[span * PLACES + spot(place), :QROWS, :] for place in range(PLACES)], axis=0
        )
        scores = lax.dot_general(
            keys[:seen], own, (((1,), (1,)), ((), ())), preferred_element_type=jnp.float32
        )
        state.append(scores)
    soft = []
    for scores in state:
        highest = jnp.max(scores, axis=0, keepdims=True) * EXP2_SCALE
        weights = jnp.exp2(scores * EXP2_SCALE - highest)
        total = jnp.sum(weights, axis=0, keepdims=True)
        soft.append((highest, weights.astype(jnp.bfloat16), total))
    for turn, span in enumerate(spans):
        seen = (turn + 1) * KBLOCK
        highest, weights, total = soft[turn]
        mixed = lax.dot_general(
            weights, values[:seen], (((0,), (0,)), ((), ())), preferred_element_type=jnp.float32
        )
        mixed = (mixed * jnp.transpose(jnp.broadcast_to(1.0 / total, (HEAD_DIM, QBLOCK)))).astype(jnp.bfloat16)
        terms = [t.astype(jnp.float32) for t in split_three(highest + jnp.log2(total))]
        stat = [t[:, half * HEAD_DIM : (half + 1) * HEAD_DIM] for half in range(2) for t in terms]
        stat = jnp.concatenate(
            stat + [jnp.zeros((STATS - len(stat), HEAD_DIM), jnp.float32)], axis=0
        )
        for core in range(CORES):
            for ring in range(RING):
                source = (ring * CORES + core) * CHUNK
                out_ref[span * CORES + core, ring * CHUNK : (ring + 1) * CHUNK, :] = mixed[
                    source : source + CHUNK
                ]
            out_ref[span * CORES + core, RING * CHUNK :, :] = stat.astype(jnp.bfloat16)


def merge_kernel(parts_ref, out_ref, turn_ref):
    core = lax.axis_index("core")
    slots = (core, CORES - 1 - core)
    rows = []
    for half in range(2):
        for slot in slots:
            for s in range(SPANS):
                stats = parts_ref[s * CORES + slot, RING * CHUNK :, :].astype(jnp.float32)
                first = 3 * half
                rows.append(stats[first : first + 1] + stats[first + 1 : first + 2] + stats[first + 2 : first + 3])
    pad = jnp.zeros((HEAD_DIM - len(rows), HEAD_DIM), jnp.float32)
    turn_ref[...] = jnp.transpose(jnp.concatenate(rows + [pad], axis=0))
    for ring in range(RING):
        half, inner = divmod(ring, HEAD_DIM // (CORES * CHUNK))
        begin = pl.multiple_of((inner * CORES + core) * CHUNK, CHUNK)
        mine = turn_ref[pl.ds(begin, CHUNK), :]
        for i, slot in enumerate(slots):
            first = (half * CORES + i) * SPANS
            cols = [mine[:, first + s : first + s + 1] for s in range(SPANS)]
            highest = functools.reduce(jnp.maximum, cols)
            shares = [jnp.exp2(c - highest) for c in cols]
            total = functools.reduce(jnp.add, shares)
            mixed = jnp.zeros((CHUNK, HEAD_DIM), jnp.float32)
            for s in range(SPANS):
                part = parts_ref[s * CORES + slot, ring * CHUNK : (ring + 1) * CHUNK, :]
                mixed = mixed + part.astype(jnp.float32) * (shares[s] / total)
            mixed = mixed.astype(jnp.bfloat16)
            lanes = slice(i * HEAD_DIM, (i + 1) * HEAD_DIM)
            for place in range(PLACES):
                side = side_of(place)
                out_ref[place, ring * QROWS : (ring + 1) * QROWS, lanes] = mixed[
                    side * QROWS : (side + 1) * QROWS
                ]


def project_kernel(rows_ref, own_ref, other_ref, theirs_ref, theirs_other_ref, out_ref):
    side = lax.axis_index("side")
    left = [
        jnp.concatenate(
            [
                jnp.concatenate(
                    [rows_ref[head * BLOCKS + b, :, lanes] for b in range(BLOCKS)], axis=0
                )
                for head in range(HEADS_HERE)
            ],
            axis=1,
        )
        for lanes in (slice(0, HEAD_DIM), slice(HEAD_DIM, 2 * HEAD_DIM))
    ]
    for weights, target in (
        ((own_ref, other_ref), side),
        ((theirs_ref, theirs_other_ref), 1 - side),
    ):
        sums = [
            lax.dot_general(x, w[...], (((1,), (1,)), ((), ())), preferred_element_type=jnp.float32)
            for x, w in zip(left, weights)
        ]
        total = sums[0] + sums[1]
        for ring in range(RING):
            piece = jnp.concatenate(
                [
                    total[(block * RING + ring) * QROWS : (block * RING + ring + 1) * QROWS]
                    for block in range(BLOCKS)
                ],
                axis=0,
            )
            edge = piece[:, 2 * HEAD_DIM :]
            edge = jnp.concatenate([edge[: ROWS // 2], edge[ROWS // 2 :]], axis=1)
            dense = [piece[:, :HEAD_DIM], piece[:, HEAD_DIM : 2 * HEAD_DIM], edge]
            out_ref[ring * 2 + target] = jnp.concatenate(dense, axis=0).astype(jnp.bfloat16)


def finish_kernel(parts_ref, gate_ref, out_ref):
    gate = gate_ref[...]
    half, width = ROWS // 2, out_ref.shape[1] - 2 * HEAD_DIM
    for side in range(2):
        total = parts_ref[side].astype(jnp.float32)
        for ring in range(1, RING):
            total = total + parts_ref[ring * 2 + side].astype(jnp.float32)
        begin = side * ROWS
        for i in range(2):
            cols = slice(i * HEAD_DIM, (i + 1) * HEAD_DIM)
            part = total[i * ROWS : (i + 1) * ROWS] * gate[:, cols]
            out_ref[begin : begin + ROWS, cols] = part.astype(jnp.bfloat16)
        edge = total[2 * ROWS :]
        edge = jnp.concatenate([edge[:, :width], edge[:, width:]], axis=0) * gate[:, 2 * HEAD_DIM :]
        out_ref[begin : begin + ROWS, 2 * HEAD_DIM :] = edge.astype(jnp.bfloat16)


def side_of(place):
    return place // 2 % 2


def swap_sides(x):
    return lax.ppermute(x, "side", [(0, 1), (1, 0)])


def swap_cores(x):
    return lax.ppermute(x, "core", [(0, 1), (1, 0)])


def shards(queries, keys, values, out_weight, gate_table, noise_level, span_order):
    shard = (ROWS, HEADS_HERE * HEAD_DIM)
    packed = pl.pallas_call(
        pack_kernel,
        out_shape=jax.ShapeDtypeStruct((SPANS * PLACES, QROWS + 2 * KROWS, HEAD_DIM), jnp.bfloat16),
        in_specs=[HBM] * 3,
        out_specs=VMEM,
        scratch_shapes=[pltpu.VMEM(shard, jnp.bfloat16)] * 3
        + [
            pltpu.VMEM((SPANS, 2 * KROWS, shard[1]), jnp.float32),
            pltpu.SemaphoreType.DMA((3,)),
        ],
        compiler_params=params(60),
        name="pack",
    )(queries, keys, values)
    level = lax.dynamic_index_in_dim(noise_level, lax.axis_index("span"), 0, keepdims=False)
    gate_row = lax.dynamic_slice_in_dim(gate_table, level, 1, 0)
    packed, weight = lax.optimization_barrier((packed, out_weight.T))
    theirs, other = swap_sides(weight), swap_cores(weight)
    theirs_other = swap_cores(theirs)
    rows = lax.all_to_all(packed, ("span", "part", "far", "side"), 0, 0, tiled=True)
    parts = pl.pallas_call(
        attend_kernel,
        out_shape=jax.ShapeDtypeStruct((SPANS * CORES, RING * CHUNK + STATS, HEAD_DIM), jnp.bfloat16),
        in_specs=[VMEM, VMEM],
        out_specs=VMEM,
        scratch_shapes=[pltpu.VMEM((SPANS * KBLOCK, HEAD_DIM), jnp.float32)] * 2,
        compiler_params=params(),
        name="attend",
    )(span_order.reshape(1, SPANS), rows)
    parts, other, gate_row = lax.optimization_barrier((parts, other, gate_row))
    parts = lax.all_to_all(parts, ("span", "core"), 0, 0, tiled=True)
    parts, theirs, theirs_other = lax.optimization_barrier((parts, theirs, theirs_other))
    merged = pl.pallas_call(
        merge_kernel,
        out_shape=jax.ShapeDtypeStruct((PLACES, RING * QROWS, CORES * HEAD_DIM), jnp.bfloat16),
        in_specs=[VMEM],
        out_specs=VMEM,
        scratch_shapes=[pltpu.VMEM((HEAD_DIM, HEAD_DIM), jnp.float32)],
        compiler_params=params(),
        name="merge",
    )(parts)
    merged = lax.all_to_all(merged, SEQ, 0, 0, tiled=True)
    sums = pl.pallas_call(
        project_kernel,
        out_shape=jax.ShapeDtypeStruct((RING * 2, 2 * ROWS + ROWS // 2, HEAD_DIM), jnp.bfloat16),
        in_specs=[VMEM] * 5,
        out_specs=VMEM,
        compiler_params=params(),
        name="project",
    )(merged, weight, other, theirs, theirs_other)
    sums = lax.all_to_all(sums, ("ring", "side"), 0, 0, tiled=True)
    return pl.pallas_call(
        finish_kernel,
        out_shape=jax.ShapeDtypeStruct((2 * ROWS, out_weight.shape[1]), jnp.bfloat16),
        in_specs=[VMEM, VMEM],
        out_specs=VMEM,
        compiler_params=params(),
        name="finish",
    )(sums, gate_row)


def solution(mesh):
    fine = jax.sharding.Mesh(
        mesh.devices.reshape(SPANS, RING, CORES, 4, 2, 2),
        ("span", "ring", "core", "far", "side", "part"),
    )
    return jax.shard_map(
        shards,
        mesh=fine,
        in_specs=(
            P(("span",) + SEQ, HEAD),
            P(("span",) + SEQ, HEAD),
            P(("span",) + SEQ, HEAD),
            P(HEAD, SEQ),
            P(None, SEQ),
            P(),
            P(),
        ),
        out_specs=P(("span",) + HEAD, SEQ),
        check_vma=False,
    )
```

```python
import functools
import math

import jax
import jax.numpy as jnp
from jax import lax
from jax.experimental import pallas as pl
from jax.experimental.pallas import tpu as pltpu
from jax.sharding import PartitionSpec as P

HEAD_DIM = 128
SPANS = 4
RING, CORES = 4, 2
GROUPS = 8
HEADS_HERE = 5
BLOCKS = 3
PLACES = 16
ROWS = 48
QROWS = ROWS // BLOCKS
KROWS = ROWS // SPANS
KBLOCK = PLACES * KROWS
QBLOCK = PLACES * QROWS
CHUNK = 2 * QROWS
STATS = 8
HEAD = ("ring", "core")
SEQ = ("far", "side", "part")
EXP2_SCALE = math.log2(math.e) / math.sqrt(HEAD_DIM)
VMEM = pl.BlockSpec(memory_space=pltpu.VMEM)
HBM = pl.BlockSpec(memory_space=pltpu.HBM)


def params(mib=24):
    return pltpu.CompilerParams(vmem_limit_bytes=mib * 2**20)


def spot(place):
    return place % 2 * (PLACES // 2) + place // 2


def pack_kernel(q_hbm, k_hbm, v_hbm, out_ref, q_ref, k_ref, v_ref, kv_ref, sems):
    copies = [
        pltpu.make_async_copy(source, target, sems.at[i])
        for i, (source, target) in enumerate(((q_hbm, q_ref), (k_hbm, k_ref), (v_hbm, v_ref)))
    ]
    for copy in copies:
        copy.start()
    for span in range(SPANS):
        for place in range(HEADS_HERE * BLOCKS, PLACES):
            out_ref[span * PLACES + spot(place)] = jnp.zeros(out_ref.shape[1:], out_ref.dtype)
    copies[0].wait()
    for head in range(HEADS_HERE):
        cols = slice(head * HEAD_DIM, (head + 1) * HEAD_DIM)
        for block in range(BLOCKS):
            part = q_ref[block * QROWS : (block + 1) * QROWS, cols]
            for span in range(SPANS):
                out_ref[span * PLACES + spot(head * BLOCKS + block), :QROWS, :] = part
    copies[1].wait()
    copies[2].wait()
    key_rows = k_ref[...].astype(jnp.float32)
    value_rows = v_ref[...].astype(jnp.float32)
    for span in range(SPANS):
        kv_ref[span, :KROWS, :] = key_rows[span * KROWS : (span + 1) * KROWS]
        kv_ref[span, KROWS:, :] = value_rows[span * KROWS : (span + 1) * KROWS]
    for span in range(SPANS):
        both = kv_ref[span].astype(jnp.bfloat16)
        for head in range(HEADS_HERE):
            part = both[:, head * HEAD_DIM : (head + 1) * HEAD_DIM]
            for block in range(BLOCKS):
                out_ref[span * PLACES + spot(head * BLOCKS + block), QROWS:, :] = part


def split_three(x):
    high = x.astype(jnp.bfloat16)
    rest = x - high.astype(jnp.float32)
    middle = rest.astype(jnp.bfloat16)
    low = (rest - middle.astype(jnp.float32)).astype(jnp.bfloat16)
    return high, middle, low


def attend_kernel(order_ref, rows_ref, out_ref, keys_ref, values_ref):
    line = order_ref[...]
    order = [line[0, i] for i in range(SPANS)]
    spans = []
    for turn in range(SPANS):
        span = jnp.int32(0)
        for other in range(1, SPANS):
            span = span + jnp.where(order[other] == turn, other, 0)
        span = jnp.minimum(span, SPANS - 1)
        spans.append(span)
        for place in range(PLACES):
            both = rows_ref[span * PLACES + place, QROWS:, :].astype(jnp.float32)
            target = turn * KBLOCK + place * KROWS
            keys_ref[target : target + KROWS, :] = both[:KROWS]
            values_ref[target : target + KROWS, :] = both[KROWS:]
    keys = keys_ref[...].astype(jnp.bfloat16)
    values = values_ref[...].astype(jnp.bfloat16)
    state = []
    for turn, span in enumerate(spans):
        seen = (turn + 1) * KBLOCK
        own = jnp.concatenate(
            [rows_ref[span * PLACES + spot(place), :QROWS, :] for place in range(PLACES)], axis=0
        )
        scores = lax.dot_general(
            keys[:seen], own, (((1,), (1,)), ((), ())), preferred_element_type=jnp.float32
        )
        state.append(scores)
    soft = []
    for scores in state:
        highest = jnp.max(scores, axis=0, keepdims=True) * EXP2_SCALE
        weights = jnp.exp2(scores * EXP2_SCALE - highest)
        total = jnp.sum(weights, axis=0, keepdims=True)
        soft.append((highest, weights.astype(jnp.bfloat16), total))
    for turn, span in enumerate(spans):
        seen = (turn + 1) * KBLOCK
        highest, weights, total = soft[turn]
        mixed = lax.dot_general(
            weights, values[:seen], (((0,), (0,)), ((), ())), preferred_element_type=jnp.float32
        )
        mixed = (mixed * jnp.transpose(jnp.broadcast_to(1.0 / total, (HEAD_DIM, QBLOCK)))).astype(jnp.bfloat16)
        terms = [t.astype(jnp.float32) for t in split_three(highest + jnp.log2(total))]
        stat = [t[:, half * HEAD_DIM : (half + 1) * HEAD_DIM] for half in range(2) for t in terms]
        stat = jnp.concatenate(
            stat + [jnp.zeros((STATS - len(stat), HEAD_DIM), jnp.float32)], axis=0
        )
        for core in range(CORES):
            for ring in range(RING):
                source = (ring * CORES + core) * CHUNK
                out_ref[span * CORES + core, ring * CHUNK : (ring + 1) * CHUNK, :] = mixed[
                    source : source + CHUNK
                ]
            out_ref[span * CORES + core, RING * CHUNK :, :] = stat.astype(jnp.bfloat16)


def berth(place):
    return place // 4 * 4 + place % 2 * 2 + place // 2 % 2


def merge_kernel(parts_ref, out_ref, turn_ref):
    core = lax.axis_index("core")
    slots = (core, CORES - 1 - core)
    rows = []
    for half in range(2):
        for slot in slots:
            for s in range(SPANS):
                stats = parts_ref[s * CORES + slot, RING * CHUNK :, :].astype(jnp.float32)
                first = 3 * half
                rows.append(stats[first : first + 1] + stats[first + 1 : first + 2] + stats[first + 2 : first + 3])
    pad = jnp.zeros((HEAD_DIM - len(rows), HEAD_DIM), jnp.float32)
    turn_ref[...] = jnp.transpose(jnp.concatenate(rows + [pad], axis=0))
    for ring in range(RING):
        half, inner = divmod(ring, HEAD_DIM // (CORES * CHUNK))
        begin = pl.multiple_of((inner * CORES + core) * CHUNK, CHUNK)
        mine = turn_ref[pl.ds(begin, CHUNK), :]
        for i, slot in enumerate(slots):
            first = (half * CORES + i) * SPANS
            cols = [mine[:, first + s : first + s + 1] for s in range(SPANS)]
            highest = functools.reduce(jnp.maximum, cols)
            shares = [jnp.exp2(c - highest) for c in cols]
            total = functools.reduce(jnp.add, shares)
            mixed = jnp.zeros((CHUNK, HEAD_DIM), jnp.float32)
            for s in range(SPANS):
                part = parts_ref[s * CORES + slot, ring * CHUNK : (ring + 1) * CHUNK, :]
                mixed = mixed + part.astype(jnp.float32) * (shares[s] / total)
            mixed = mixed.astype(jnp.bfloat16)
            lanes = slice(i * HEAD_DIM, (i + 1) * HEAD_DIM)
            for place in range(PLACES):
                side = side_of(place)
                out_ref[berth(place), ring * QROWS : (ring + 1) * QROWS, lanes] = mixed[
                    side * QROWS : (side + 1) * QROWS
                ]


def project_kernel(rows_ref, own_ref, other_ref, theirs_ref, theirs_other_ref, out_ref):
    side = lax.axis_index("side")
    left = [
        jnp.concatenate(
            [
                jnp.concatenate(
                    [rows_ref[berth(head * BLOCKS + b), :, lanes] for b in range(BLOCKS)], axis=0
                )
                for head in range(HEADS_HERE)
            ],
            axis=1,
        )
        for lanes in (slice(0, HEAD_DIM), slice(HEAD_DIM, 2 * HEAD_DIM))
    ]
    for weights, target in (
        ((own_ref, other_ref), side),
        ((theirs_ref, theirs_other_ref), 1 - side),
    ):
        sums = [
            lax.dot_general(x, w[...], (((1,), (1,)), ((), ())), preferred_element_type=jnp.float32)
            for x, w in zip(left, weights)
        ]
        total = sums[0] + sums[1]
        for ring in range(RING):
            piece = jnp.concatenate(
                [
                    total[(block * RING + ring) * QROWS : (block * RING + ring + 1) * QROWS]
                    for block in range(BLOCKS)
                ],
                axis=0,
            )
            edge = piece[:, 2 * HEAD_DIM :]
            edge = jnp.concatenate([edge[: ROWS // 2], edge[ROWS // 2 :]], axis=1)
            dense = [piece[:, :HEAD_DIM], piece[:, HEAD_DIM : 2 * HEAD_DIM], edge]
            out_ref[ring * 2 + target] = jnp.concatenate(dense, axis=0).astype(jnp.bfloat16)


def finish_kernel(parts_ref, gate_ref, out_ref):
    gate = gate_ref[...]
    half, width = ROWS // 2, out_ref.shape[1] - 2 * HEAD_DIM
    for side in range(2):
        total = parts_ref[side].astype(jnp.float32)
        for ring in range(1, RING):
            total = total + parts_ref[ring * 2 + side].astype(jnp.float32)
        begin = side * ROWS
        for i in range(2):
            cols = slice(i * HEAD_DIM, (i + 1) * HEAD_DIM)
            part = total[i * ROWS : (i + 1) * ROWS] * gate[:, cols]
            out_ref[begin : begin + ROWS, cols] = part.astype(jnp.bfloat16)
        edge = total[2 * ROWS :]
        edge = jnp.concatenate([edge[:, :width], edge[:, width:]], axis=0) * gate[:, 2 * HEAD_DIM :]
        out_ref[begin : begin + ROWS, 2 * HEAD_DIM :] = edge.astype(jnp.bfloat16)


def side_of(place):
    return place // 2 % 2


def swap_sides(x):
    return lax.ppermute(x, "side", [(0, 1), (1, 0)])


def swap_cores(x):
    return lax.ppermute(x, "core", [(0, 1), (1, 0)])


def shards(queries, keys, values, out_weight, gate_table, noise_level, span_order):
    shard = (ROWS, HEADS_HERE * HEAD_DIM)
    packed = pl.pallas_call(
        pack_kernel,
        out_shape=jax.ShapeDtypeStruct((SPANS * PLACES, QROWS + 2 * KROWS, HEAD_DIM), jnp.bfloat16),
        in_specs=[HBM] * 3,
        out_specs=VMEM,
        scratch_shapes=[pltpu.VMEM(shard, jnp.bfloat16)] * 3
        + [
            pltpu.VMEM((SPANS, 2 * KROWS, shard[1]), jnp.float32),
            pltpu.SemaphoreType.DMA((3,)),
        ],
        compiler_params=params(60),
        name="pack",
    )(queries, keys, values)
    level = lax.dynamic_index_in_dim(noise_level, lax.axis_index("span"), 0, keepdims=False)
    gate_row = lax.dynamic_slice_in_dim(gate_table, level, 1, 0)
    packed, weight = lax.optimization_barrier((packed, out_weight.T))
    theirs, other = swap_sides(weight), swap_cores(weight)
    theirs_other = swap_cores(theirs)
    rows = lax.all_to_all(packed, ("span", "part", "far", "side"), 0, 0, tiled=True)
    parts = pl.pallas_call(
        attend_kernel,
        out_shape=jax.ShapeDtypeStruct((SPANS * CORES, RING * CHUNK + STATS, HEAD_DIM), jnp.bfloat16),
        in_specs=[VMEM, VMEM],
        out_specs=VMEM,
        scratch_shapes=[pltpu.VMEM((SPANS * KBLOCK, HEAD_DIM), jnp.float32)] * 2,
        compiler_params=params(),
        name="attend",
    )(span_order.reshape(1, SPANS), rows)
    parts, other, gate_row = lax.optimization_barrier((parts, other, gate_row))
    parts = lax.all_to_all(parts, ("span", "core"), 0, 0, tiled=True)
    parts, theirs, theirs_other = lax.optimization_barrier((parts, theirs, theirs_other))
    merged = pl.pallas_call(
        merge_kernel,
        out_shape=jax.ShapeDtypeStruct((PLACES, RING * QROWS, CORES * HEAD_DIM), jnp.bfloat16),
        in_specs=[VMEM],
        out_specs=VMEM,
        scratch_shapes=[pltpu.VMEM((HEAD_DIM, HEAD_DIM), jnp.float32)],
        compiler_params=params(),
        name="merge",
    )(parts)
    merged = lax.all_to_all(merged, ("far", "part", "side"), 0, 0, tiled=True)
    sums = pl.pallas_call(
        project_kernel,
        out_shape=jax.ShapeDtypeStruct((RING * 2, 2 * ROWS + ROWS // 2, HEAD_DIM), jnp.bfloat16),
        in_specs=[VMEM] * 5,
        out_specs=VMEM,
        compiler_params=params(),
        name="project",
    )(merged, weight, other, theirs, theirs_other)
    sums = lax.all_to_all(sums, ("ring", "side"), 0, 0, tiled=True)
    return pl.pallas_call(
        finish_kernel,
        out_shape=jax.ShapeDtypeStruct((2 * ROWS, out_weight.shape[1]), jnp.bfloat16),
        in_specs=[VMEM, VMEM],
        out_specs=VMEM,
        compiler_params=params(),
        name="finish",
    )(sums, gate_row)


def solution(mesh):
    fine = jax.sharding.Mesh(
        mesh.devices.reshape(SPANS, RING, CORES, 4, 2, 2),
        ("span", "ring", "core", "far", "side", "part"),
    )
    return jax.shard_map(
        shards,
        mesh=fine,
        in_specs=(
            P(("span",) + SEQ, HEAD),
            P(("span",) + SEQ, HEAD),
            P(("span",) + SEQ, HEAD),
            P(HEAD, SEQ),
            P(None, SEQ),
            P(),
            P(),
        ),
        out_specs=P(("span",) + HEAD, SEQ),
        check_vma=False,
    )
```

```python
import functools
import math

import jax
import jax.numpy as jnp
from jax import lax
from jax.experimental import pallas as pl
from jax.experimental.pallas import tpu as pltpu
from jax.sharding import PartitionSpec as P

HEAD_DIM = 128
SPANS = 4
RING, CORES = 4, 2
GROUPS = 8
HEADS_HERE = 5
BLOCKS = 3
PLACES = 16
ROWS = 48
QROWS = ROWS // BLOCKS
KROWS = ROWS // SPANS
KBLOCK = PLACES * KROWS
QBLOCK = PLACES * QROWS
CHUNK = 2 * QROWS
STATS = 8
HEAD = ("ring", "core")
SEQ = ("far", "side", "part")
EXP2_SCALE = math.log2(math.e) / math.sqrt(HEAD_DIM)
VMEM = pl.BlockSpec(memory_space=pltpu.VMEM)
HBM = pl.BlockSpec(memory_space=pltpu.HBM)


def params(mib=24):
    return pltpu.CompilerParams(vmem_limit_bytes=mib * 2**20)


def spot(place):
    return place % 2 * (PLACES // 2) + place // 2


def pack_kernel(q_hbm, k_hbm, v_hbm, out_ref, q_ref, k_ref, v_ref, kv_ref, sems):
    copies = [
        pltpu.make_async_copy(source, target, sems.at[i])
        for i, (source, target) in enumerate(((q_hbm, q_ref), (k_hbm, k_ref), (v_hbm, v_ref)))
    ]
    for copy in copies:
        copy.start()
    for span in range(SPANS):
        for place in range(HEADS_HERE * BLOCKS, PLACES):
            out_ref[span * PLACES + spot(place)] = jnp.zeros(out_ref.shape[1:], out_ref.dtype)
    copies[0].wait()
    for head in range(HEADS_HERE):
        cols = slice(head * HEAD_DIM, (head + 1) * HEAD_DIM)
        for block in range(BLOCKS):
            part = q_ref[block * QROWS : (block + 1) * QROWS, cols]
            for span in range(SPANS):
                out_ref[span * PLACES + spot(head * BLOCKS + block), :QROWS, :] = part
    copies[1].wait()
    copies[2].wait()
    key_rows = k_ref[...].astype(jnp.float32)
    value_rows = v_ref[...].astype(jnp.float32)
    for span in range(SPANS):
        kv_ref[span, :KROWS, :] = key_rows[span * KROWS : (span + 1) * KROWS]
        kv_ref[span, KROWS:, :] = value_rows[span * KROWS : (span + 1) * KROWS]
    for span in range(SPANS):
        both = kv_ref[span].astype(jnp.bfloat16)
        for head in range(HEADS_HERE):
            part = both[:, head * HEAD_DIM : (head + 1) * HEAD_DIM]
            for block in range(BLOCKS):
                out_ref[span * PLACES + spot(head * BLOCKS + block), QROWS:, :] = part


def split_three(x):
    high = x.astype(jnp.bfloat16)
    rest = x - high.astype(jnp.float32)
    middle = rest.astype(jnp.bfloat16)
    low = (rest - middle.astype(jnp.float32)).astype(jnp.bfloat16)
    return high, middle, low


def attend_kernel(order_ref, rows_ref, out_ref, keys_ref, values_ref):
    line = order_ref[...]
    order = [line[0, i] for i in range(SPANS)]
    spans = []
    for turn in range(SPANS):
        span = jnp.int32(0)
        for other in range(1, SPANS):
            span = span + jnp.where(order[other] == turn, other, 0)
        span = jnp.minimum(span, SPANS - 1)
        spans.append(span)
        for place in range(PLACES):
            both = rows_ref[span * PLACES + place, QROWS:, :].astype(jnp.float32)
            target = turn * KBLOCK + place * KROWS
            keys_ref[target : target + KROWS, :] = both[:KROWS]
            values_ref[target : target + KROWS, :] = both[KROWS:]
    keys = keys_ref[...].astype(jnp.bfloat16)
    values = values_ref[...].astype(jnp.bfloat16)
    state = []
    for turn, span in enumerate(spans):
        seen = (turn + 1) * KBLOCK
        own = jnp.concatenate(
            [rows_ref[span * PLACES + spot(place), :QROWS, :] for place in range(PLACES)], axis=0
        )
        scores = lax.dot_general(
            keys[:seen], own, (((1,), (1,)), ((), ())), preferred_element_type=jnp.float32
        )
        state.append(scores)
    soft = []
    for scores in state:
        highest = jnp.max(scores, axis=0, keepdims=True) * EXP2_SCALE
        weights = jnp.exp2(scores * EXP2_SCALE - highest)
        total = jnp.sum(weights, axis=0, keepdims=True)
        soft.append((highest, weights.astype(jnp.bfloat16), total))
    for turn, span in enumerate(spans):
        seen = (turn + 1) * KBLOCK
        highest, weights, total = soft[turn]
        mixed = lax.dot_general(
            weights, values[:seen], (((0,), (0,)), ((), ())), preferred_element_type=jnp.float32
        )
        mixed = (mixed * jnp.transpose(jnp.broadcast_to(1.0 / total, (HEAD_DIM, QBLOCK)))).astype(jnp.bfloat16)
        terms = [t.astype(jnp.float32) for t in split_three(highest + jnp.log2(total))]
        stat = [t[:, half * HEAD_DIM : (half + 1) * HEAD_DIM] for half in range(2) for t in terms]
        stat = jnp.concatenate(
            stat + [jnp.zeros((STATS - len(stat), HEAD_DIM), jnp.float32)], axis=0
        )
        for core in range(CORES):
            for ring in range(RING):
                source = (ring * CORES + core) * CHUNK
                out_ref[core * SPANS + span, ring * CHUNK : (ring + 1) * CHUNK, :] = mixed[
                    source : source + CHUNK
                ]
            out_ref[core * SPANS + span, RING * CHUNK :, :] = stat.astype(jnp.bfloat16)


def berth(place):
    return place // 4 * 4 + place % 2 * 2 + place // 2 % 2


def merge_kernel(parts_ref, out_ref, turn_ref):
    core = lax.axis_index("core")
    slots = (core, CORES - 1 - core)
    rows = []
    for half in range(2):
        for slot in slots:
            for s in range(SPANS):
                stats = parts_ref[slot * SPANS + s, RING * CHUNK :, :].astype(jnp.float32)
                first = 3 * half
                rows.append(stats[first : first + 1] + stats[first + 1 : first + 2] + stats[first + 2 : first + 3])
    pad = jnp.zeros((HEAD_DIM - len(rows), HEAD_DIM), jnp.float32)
    turn_ref[...] = jnp.transpose(jnp.concatenate(rows + [pad], axis=0))
    for ring in range(RING):
        half, inner = divmod(ring, HEAD_DIM // (CORES * CHUNK))
        begin = pl.multiple_of((inner * CORES + core) * CHUNK, CHUNK)
        mine = turn_ref[pl.ds(begin, CHUNK), :]
        for i, slot in enumerate(slots):
            first = (half * CORES + i) * SPANS
            cols = [mine[:, first + s : first + s + 1] for s in range(SPANS)]
            highest = functools.reduce(jnp.maximum, cols)
            shares = [jnp.exp2(c - highest) for c in cols]
            total = functools.reduce(jnp.add, shares)
            mixed = jnp.zeros((CHUNK, HEAD_DIM), jnp.float32)
            for s in range(SPANS):
                part = parts_ref[slot * SPANS + s, ring * CHUNK : (ring + 1) * CHUNK, :]
                mixed = mixed + part.astype(jnp.float32) * (shares[s] / total)
            mixed = mixed.astype(jnp.bfloat16)
            lanes = slice(i * HEAD_DIM, (i + 1) * HEAD_DIM)
            for place in range(PLACES):
                side = side_of(place)
                out_ref[berth(place), ring * QROWS : (ring + 1) * QROWS, lanes] = mixed[
                    side * QROWS : (side + 1) * QROWS
                ]


def project_kernel(rows_ref, own_ref, other_ref, theirs_ref, theirs_other_ref, out_ref):
    side = lax.axis_index("side")
    left = [
        jnp.concatenate(
            [
                jnp.concatenate(
                    [rows_ref[berth(head * BLOCKS + b), :, lanes] for b in range(BLOCKS)], axis=0
                )
                for head in range(HEADS_HERE)
            ],
            axis=1,
        )
        for lanes in (slice(0, HEAD_DIM), slice(HEAD_DIM, 2 * HEAD_DIM))
    ]
    for weights, target in (
        ((own_ref, other_ref), side),
        ((theirs_ref, theirs_other_ref), 1 - side),
    ):
        total = lax.dot_general(
            jnp.concatenate(left, axis=1),
            jnp.concatenate([w[...] for w in weights], axis=1),
            (((1,), (1,)), ((), ())),
            preferred_element_type=jnp.float32,
        )
        for ring in range(RING):
            piece = jnp.concatenate(
                [
                    total[(block * RING + ring) * QROWS : (block * RING + ring + 1) * QROWS]
                    for block in range(BLOCKS)
                ],
                axis=0,
            )
            edge = piece[:, 2 * HEAD_DIM :]
            edge = jnp.concatenate([edge[: ROWS // 2], edge[ROWS // 2 :]], axis=1)
            dense = [piece[:, :HEAD_DIM], piece[:, HEAD_DIM : 2 * HEAD_DIM], edge]
            out_ref[target * RING + ring] = jnp.concatenate(dense, axis=0).astype(jnp.bfloat16)


def finish_kernel(parts_ref, gate_ref, out_ref):
    gate = gate_ref[...]
    half, width = ROWS // 2, out_ref.shape[1] - 2 * HEAD_DIM
    for side in range(2):
        total = parts_ref[side * RING].astype(jnp.float32)
        for ring in range(1, RING):
            total = total + parts_ref[side * RING + ring].astype(jnp.float32)
        begin = side * ROWS
        for i in range(2):
            cols = slice(i * HEAD_DIM, (i + 1) * HEAD_DIM)
            part = total[i * ROWS : (i + 1) * ROWS] * gate[:, cols]
            out_ref[begin : begin + ROWS, cols] = part.astype(jnp.bfloat16)
        edge = total[2 * ROWS :]
        edge = jnp.concatenate([edge[:, :width], edge[:, width:]], axis=0) * gate[:, 2 * HEAD_DIM :]
        out_ref[begin : begin + ROWS, 2 * HEAD_DIM :] = edge.astype(jnp.bfloat16)


def side_of(place):
    return place // 2 % 2


def swap_sides(x):
    return lax.ppermute(x, "side", [(0, 1), (1, 0)])


def swap_cores(x):
    return lax.ppermute(x, "core", [(0, 1), (1, 0)])


def shards(queries, keys, values, out_weight, gate_table, noise_level, span_order):
    shard = (ROWS, HEADS_HERE * HEAD_DIM)
    packed = pl.pallas_call(
        pack_kernel,
        out_shape=jax.ShapeDtypeStruct((SPANS * PLACES, QROWS + 2 * KROWS, HEAD_DIM), jnp.bfloat16),
        in_specs=[HBM] * 3,
        out_specs=VMEM,
        scratch_shapes=[pltpu.VMEM(shard, jnp.bfloat16)] * 3
        + [
            pltpu.VMEM((SPANS, 2 * KROWS, shard[1]), jnp.float32),
            pltpu.SemaphoreType.DMA((3,)),
        ],
        compiler_params=params(60),
        name="pack",
    )(queries, keys, values)
    level = lax.dynamic_index_in_dim(noise_level, lax.axis_index("span"), 0, keepdims=False)
    gate_row = lax.dynamic_slice_in_dim(gate_table, level, 1, 0)
    packed, weight = lax.optimization_barrier((packed, out_weight.T))
    theirs, other = swap_sides(weight), swap_cores(weight)
    theirs_other = swap_cores(theirs)
    rows = lax.all_to_all(packed, ("span", "part", "far", "side"), 0, 0, tiled=True)
    parts = pl.pallas_call(
        attend_kernel,
        out_shape=jax.ShapeDtypeStruct((SPANS * CORES, RING * CHUNK + STATS, HEAD_DIM), jnp.bfloat16),
        in_specs=[VMEM, VMEM],
        out_specs=VMEM,
        scratch_shapes=[pltpu.VMEM((SPANS * KBLOCK, HEAD_DIM), jnp.float32)] * 2,
        compiler_params=params(),
        name="attend",
    )(span_order.reshape(1, SPANS), rows)
    parts, other, gate_row = lax.optimization_barrier((parts, other, gate_row))
    parts = lax.all_to_all(parts, ("core", "span"), 0, 0, tiled=True)
    parts, theirs, theirs_other = lax.optimization_barrier((parts, theirs, theirs_other))
    merged = pl.pallas_call(
        merge_kernel,
        out_shape=jax.ShapeDtypeStruct((PLACES, RING * QROWS, CORES * HEAD_DIM), jnp.bfloat16),
        in_specs=[VMEM],
        out_specs=VMEM,
        scratch_shapes=[pltpu.VMEM((HEAD_DIM, HEAD_DIM), jnp.float32)],
        compiler_params=params(),
        name="merge",
    )(parts)
    merged = lax.all_to_all(merged, ("far", "part", "side"), 0, 0, tiled=True)
    sums = pl.pallas_call(
        project_kernel,
        out_shape=jax.ShapeDtypeStruct((RING * 2, 2 * ROWS + ROWS // 2, HEAD_DIM), jnp.bfloat16),
        in_specs=[VMEM] * 5,
        out_specs=VMEM,
        compiler_params=params(),
        name="project",
    )(merged, weight, other, theirs, theirs_other)
    sums = lax.all_to_all(sums, ("side", "ring"), 0, 0, tiled=True)
    return pl.pallas_call(
        finish_kernel,
        out_shape=jax.ShapeDtypeStruct((2 * ROWS, out_weight.shape[1]), jnp.bfloat16),
        in_specs=[VMEM, VMEM],
        out_specs=VMEM,
        compiler_params=params(),
        name="finish",
    )(sums, gate_row)


def solution(mesh):
    fine = jax.sharding.Mesh(
        mesh.devices.reshape(SPANS, RING, CORES, 4, 2, 2),
        ("span", "ring", "core", "far", "side", "part"),
    )
    return jax.shard_map(
        shards,
        mesh=fine,
        in_specs=(
            P(("span",) + SEQ, HEAD),
            P(("span",) + SEQ, HEAD),
            P(("span",) + SEQ, HEAD),
            P(HEAD, SEQ),
            P(None, SEQ),
            P(),
            P(),
        ),
        out_specs=P(("span",) + HEAD, SEQ),
        check_vma=False,
    )
```

```python
import functools
import math

import jax
import jax.numpy as jnp
from jax import lax
from jax.experimental import pallas as pl
from jax.experimental.pallas import tpu as pltpu
from jax.sharding import PartitionSpec as P

HEAD_DIM = 128
SPANS = 4
RING, CORES = 4, 2
GROUPS = 8
HEADS_HERE = 5
BLOCKS = 3
PLACES = 16
ROWS = 48
QROWS = ROWS // BLOCKS
KROWS = ROWS // SPANS
KBLOCK = PLACES * KROWS
QBLOCK = PLACES * QROWS
CHUNK = 2 * QROWS
STATS = 8
HEAD = ("ring", "core")
SEQ = ("far", "side", "part")
EXP2_SCALE = math.log2(math.e) / math.sqrt(HEAD_DIM)
VMEM = pl.BlockSpec(memory_space=pltpu.VMEM)
HBM = pl.BlockSpec(memory_space=pltpu.HBM)


def params(mib=24):
    return pltpu.CompilerParams(vmem_limit_bytes=mib * 2**20)


def pack_kernel(q_hbm, k_hbm, v_hbm, out_ref, q_ref, k_ref, v_ref, kv_ref, sems):
    copies = [
        pltpu.make_async_copy(source, target, sems.at[i])
        for i, (source, target) in enumerate(((q_hbm, q_ref), (k_hbm, k_ref), (v_hbm, v_ref)))
    ]
    for copy in copies:
        copy.start()
    for span in range(SPANS):
        for place in range(HEADS_HERE * BLOCKS, PLACES):
            out_ref[place * SPANS + span] = jnp.zeros(out_ref.shape[1:], out_ref.dtype)
    copies[0].wait()
    for head in range(HEADS_HERE):
        cols = slice(head * HEAD_DIM, (head + 1) * HEAD_DIM)
        for block in range(BLOCKS):
            part = q_ref[block * QROWS : (block + 1) * QROWS, cols]
            for span in range(SPANS):
                out_ref[(head * BLOCKS + block) * SPANS + span, :QROWS, :] = part
    copies[1].wait()
    copies[2].wait()
    key_rows = k_ref[...].astype(jnp.float32)
    value_rows = v_ref[...].astype(jnp.float32)
    for span in range(SPANS):
        kv_ref[span, :KROWS, :] = key_rows[span * KROWS : (span + 1) * KROWS]
        kv_ref[span, KROWS:, :] = value_rows[span * KROWS : (span + 1) * KROWS]
    for span in range(SPANS):
        both = kv_ref[span].astype(jnp.bfloat16)
        for head in range(HEADS_HERE):
            part = both[:, head * HEAD_DIM : (head + 1) * HEAD_DIM]
            for block in range(BLOCKS):
                out_ref[(head * BLOCKS + block) * SPANS + span, QROWS:, :] = part


def split_three(x):
    high = x.astype(jnp.bfloat16)
    rest = x - high.astype(jnp.float32)
    middle = rest.astype(jnp.bfloat16)
    low = (rest - middle.astype(jnp.float32)).astype(jnp.bfloat16)
    return high, middle, low


def attend_kernel(order_ref, rows_ref, out_ref, keys_ref, values_ref):
    line = order_ref[...]
    order = [line[0, i] for i in range(SPANS)]
    spans = []
    for turn in range(SPANS):
        span = jnp.int32(0)
        for other in range(1, SPANS):
            span = span + jnp.where(order[other] == turn, other, 0)
        span = jnp.minimum(span, SPANS - 1)
        spans.append(span)
        for place in range(PLACES):
            both = rows_ref[place * SPANS + span, QROWS:, :].astype(jnp.float32)
            target = turn * KBLOCK + place * KROWS
            keys_ref[target : target + KROWS, :] = both[:KROWS]
            values_ref[target : target + KROWS, :] = both[KROWS:]
    keys = keys_ref[...].astype(jnp.bfloat16)
    values = values_ref[...].astype(jnp.bfloat16)
    state = []
    for turn, span in enumerate(spans):
        seen = (turn + 1) * KBLOCK
        own = jnp.concatenate(
            [rows_ref[place * SPANS + span, :QROWS, :] for place in range(PLACES)], axis=0
        )
        scores = lax.dot_general(
            keys[:seen], own, (((1,), (1,)), ((), ())), preferred_element_type=jnp.float32
        )
        state.append(scores)
    soft = []
    for scores in state:
        highest = jnp.max(scores, axis=0, keepdims=True) * EXP2_SCALE
        weights = jnp.exp2(scores * EXP2_SCALE - highest)
        total = jnp.sum(weights, axis=0, keepdims=True)
        soft.append((highest, weights.astype(jnp.bfloat16), total))
    for turn, span in enumerate(spans):
        seen = (turn + 1) * KBLOCK
        highest, weights, total = soft[turn]
        mixed = lax.dot_general(
            weights, values[:seen], (((0,), (0,)), ((), ())), preferred_element_type=jnp.float32
        )
        mixed = (mixed * jnp.transpose(jnp.broadcast_to(1.0 / total, (HEAD_DIM, QBLOCK)))).astype(jnp.bfloat16)
        terms = [t.astype(jnp.float32) for t in split_three(highest + jnp.log2(total))]
        stat = [t[:, half * HEAD_DIM : (half + 1) * HEAD_DIM] for half in range(2) for t in terms]
        stat = jnp.concatenate(
            stat + [jnp.zeros((STATS - len(stat), HEAD_DIM), jnp.float32)], axis=0
        )
        for core in range(CORES):
            for ring in range(RING):
                source = (ring * CORES + core) * CHUNK
                out_ref[core * SPANS + span, ring * CHUNK : (ring + 1) * CHUNK, :] = mixed[
                    source : source + CHUNK
                ]
            out_ref[core * SPANS + span, RING * CHUNK :, :] = stat.astype(jnp.bfloat16)


def berth(place):
    return place // 4 * 4 + place % 2 * 2 + place // 2 % 2


def merge_kernel(parts_ref, out_ref, turn_ref):
    core = lax.axis_index("core")
    slots = (core, CORES - 1 - core)
    rows = []
    for half in range(2):
        for slot in slots:
            for s in range(SPANS):
                stats = parts_ref[slot * SPANS + s, RING * CHUNK :, :].astype(jnp.float32)
                first = 3 * half
                rows.append(stats[first : first + 1] + stats[first + 1 : first + 2] + stats[first + 2 : first + 3])
    pad = jnp.zeros((HEAD_DIM - len(rows), HEAD_DIM), jnp.float32)
    turn_ref[...] = jnp.transpose(jnp.concatenate(rows + [pad], axis=0))
    for ring in range(RING):
        half, inner = divmod(ring, HEAD_DIM // (CORES * CHUNK))
        begin = pl.multiple_of((inner * CORES + core) * CHUNK, CHUNK)
        mine = turn_ref[pl.ds(begin, CHUNK), :]
        for i, slot in enumerate(slots):
            first = (half * CORES + i) * SPANS
            cols = [mine[:, first + s : first + s + 1] for s in range(SPANS)]
            highest = functools.reduce(jnp.maximum, cols)
            shares = [jnp.exp2(c - highest) for c in cols]
            total = functools.reduce(jnp.add, shares)
            mixed = jnp.zeros((CHUNK, HEAD_DIM), jnp.float32)
            for s in range(SPANS):
                part = parts_ref[slot * SPANS + s, ring * CHUNK : (ring + 1) * CHUNK, :]
                mixed = mixed + part.astype(jnp.float32) * (shares[s] / total)
            mixed = mixed.astype(jnp.bfloat16)
            lanes = slice(i * HEAD_DIM, (i + 1) * HEAD_DIM)
            for place in range(PLACES):
                side = side_of(place)
                out_ref[berth(place), ring * QROWS : (ring + 1) * QROWS, lanes] = mixed[
                    side * QROWS : (side + 1) * QROWS
                ]


def project_kernel(rows_ref, own_ref, other_ref, theirs_ref, theirs_other_ref, out_ref):
    side = lax.axis_index("side")
    left = [
        jnp.concatenate(
            [
                jnp.concatenate(
                    [rows_ref[berth(head * BLOCKS + b), :, lanes] for b in range(BLOCKS)], axis=0
                )
                for head in range(HEADS_HERE)
            ],
            axis=1,
        )
        for lanes in (slice(0, HEAD_DIM), slice(HEAD_DIM, 2 * HEAD_DIM))
    ]
    for weights, target in (
        ((own_ref, other_ref), side),
        ((theirs_ref, theirs_other_ref), 1 - side),
    ):
        total = lax.dot_general(
            jnp.concatenate(left, axis=1),
            jnp.concatenate([w[...] for w in weights], axis=1),
            (((1,), (1,)), ((), ())),
            preferred_element_type=jnp.float32,
        )
        for ring in range(RING):
            piece = jnp.concatenate(
                [
                    total[(block * RING + ring) * QROWS : (block * RING + ring + 1) * QROWS]
                    for block in range(BLOCKS)
                ],
                axis=0,
            )
            edge = piece[:, 2 * HEAD_DIM :]
            edge = jnp.concatenate([edge[: ROWS // 2], edge[ROWS // 2 :]], axis=1)
            dense = [piece[:, :HEAD_DIM], piece[:, HEAD_DIM : 2 * HEAD_DIM], edge]
            out_ref[target * RING + ring] = jnp.concatenate(dense, axis=0).astype(jnp.bfloat16)


def finish_kernel(parts_ref, gate_ref, out_ref):
    gate = gate_ref[...]
    half, width = ROWS // 2, out_ref.shape[1] - 2 * HEAD_DIM
    for side in range(2):
        total = parts_ref[side * RING].astype(jnp.float32)
        for ring in range(1, RING):
            total = total + parts_ref[side * RING + ring].astype(jnp.float32)
        begin = side * ROWS
        for i in range(2):
            cols = slice(i * HEAD_DIM, (i + 1) * HEAD_DIM)
            part = total[i * ROWS : (i + 1) * ROWS] * gate[:, cols]
            out_ref[begin : begin + ROWS, cols] = part.astype(jnp.bfloat16)
        edge = total[2 * ROWS :]
        edge = jnp.concatenate([edge[:, :width], edge[:, width:]], axis=0) * gate[:, 2 * HEAD_DIM :]
        out_ref[begin : begin + ROWS, 2 * HEAD_DIM :] = edge.astype(jnp.bfloat16)


def side_of(place):
    return place // 2 % 2


def swap_sides(x):
    return lax.ppermute(x, "side", [(0, 1), (1, 0)])


def swap_cores(x):
    return lax.ppermute(x, "core", [(0, 1), (1, 0)])


def shards(queries, keys, values, out_weight, gate_table, noise_level, span_order):
    shard = (ROWS, HEADS_HERE * HEAD_DIM)
    packed = pl.pallas_call(
        pack_kernel,
        out_shape=jax.ShapeDtypeStruct((SPANS * PLACES, QROWS + 2 * KROWS, HEAD_DIM), jnp.bfloat16),
        in_specs=[HBM] * 3,
        out_specs=VMEM,
        scratch_shapes=[pltpu.VMEM(shard, jnp.bfloat16)] * 3
        + [
            pltpu.VMEM((SPANS, 2 * KROWS, shard[1]), jnp.float32),
            pltpu.SemaphoreType.DMA((3,)),
        ],
        compiler_params=params(60),
        name="pack",
    )(queries, keys, values)
    level = lax.dynamic_index_in_dim(noise_level, lax.axis_index("span"), 0, keepdims=False)
    gate_row = lax.dynamic_slice_in_dim(gate_table, level, 1, 0)
    packed, weight = lax.optimization_barrier((packed, out_weight.T))
    theirs, other = swap_sides(weight), swap_cores(weight)
    theirs_other = swap_cores(theirs)
    rows = lax.all_to_all(packed, SEQ + ("span",), 0, 0, tiled=True)
    parts = pl.pallas_call(
        attend_kernel,
        out_shape=jax.ShapeDtypeStruct((SPANS * CORES, RING * CHUNK + STATS, HEAD_DIM), jnp.bfloat16),
        in_specs=[VMEM, VMEM],
        out_specs=VMEM,
        scratch_shapes=[pltpu.VMEM((SPANS * KBLOCK, HEAD_DIM), jnp.float32)] * 2,
        compiler_params=params(),
        name="attend",
    )(span_order.reshape(1, SPANS), rows)
    parts, other, gate_row = lax.optimization_barrier((parts, other, gate_row))
    parts = lax.all_to_all(parts, ("core", "span"), 0, 0, tiled=True)
    parts, theirs, theirs_other = lax.optimization_barrier((parts, theirs, theirs_other))
    merged = pl.pallas_call(
        merge_kernel,
        out_shape=jax.ShapeDtypeStruct((PLACES, RING * QROWS, CORES * HEAD_DIM), jnp.bfloat16),
        in_specs=[VMEM],
        out_specs=VMEM,
        scratch_shapes=[pltpu.VMEM((HEAD_DIM, HEAD_DIM), jnp.float32)],
        compiler_params=params(),
        name="merge",
    )(parts)
    merged = lax.all_to_all(merged, ("far", "part", "side"), 0, 0, tiled=True)
    sums = pl.pallas_call(
        project_kernel,
        out_shape=jax.ShapeDtypeStruct((RING * 2, 2 * ROWS + ROWS // 2, HEAD_DIM), jnp.bfloat16),
        in_specs=[VMEM] * 5,
        out_specs=VMEM,
        compiler_params=params(),
        name="project",
    )(merged, weight, other, theirs, theirs_other)
    sums = lax.all_to_all(sums, ("side", "ring"), 0, 0, tiled=True)
    return pl.pallas_call(
        finish_kernel,
        out_shape=jax.ShapeDtypeStruct((2 * ROWS, out_weight.shape[1]), jnp.bfloat16),
        in_specs=[VMEM, VMEM],
        out_specs=VMEM,
        compiler_params=params(),
        name="finish",
    )(sums, gate_row)


def solution(mesh):
    fine = jax.sharding.Mesh(
        mesh.devices.reshape(SPANS, RING, CORES, 4, 2, 2),
        ("span", "ring", "core", "far", "side", "part"),
    )
    return jax.shard_map(
        shards,
        mesh=fine,
        in_specs=(
            P(("span",) + SEQ, HEAD),
            P(("span",) + SEQ, HEAD),
            P(("span",) + SEQ, HEAD),
            P(HEAD, SEQ),
            P(None, SEQ),
            P(),
            P(),
        ),
        out_specs=P(("span",) + HEAD, SEQ),
        check_vma=False,
    )
```

```python
import functools
import math

import jax
import jax.numpy as jnp
from jax import lax
from jax.experimental import pallas as pl
from jax.experimental.pallas import tpu as pltpu
from jax.sharding import PartitionSpec as P

HEAD_DIM = 128
SPANS = 4
RING, CORES = 4, 2
GROUPS = 8
HEADS_HERE = 5
BLOCKS = 3
PLACES = 16
ROWS = 48
QROWS = ROWS // BLOCKS
KROWS = ROWS // SPANS
KBLOCK = PLACES * KROWS
QBLOCK = PLACES * QROWS
CHUNK = 2 * QROWS
STATS = 8
HEAD = ("ring", "core")
SEQ = ("far", "side", "part")
EXP2_SCALE = math.log2(math.e) / math.sqrt(HEAD_DIM)
VMEM = pl.BlockSpec(memory_space=pltpu.VMEM)
HBM = pl.BlockSpec(memory_space=pltpu.HBM)


def params(mib=24):
    return pltpu.CompilerParams(vmem_limit_bytes=mib * 2**20)


def spot(place):
    return place % 2 * (PLACES // 2) + place // 2


def pack_kernel(q_hbm, k_hbm, v_hbm, out_ref, q_ref, k_ref, v_ref, kv_ref, sems):
    copies = [
        pltpu.make_async_copy(source, target, sems.at[i])
        for i, (source, target) in enumerate(((q_hbm, q_ref), (k_hbm, k_ref), (v_hbm, v_ref)))
    ]
    for copy in copies:
        copy.start()
    for span in range(SPANS):
        for place in range(HEADS_HERE * BLOCKS, PLACES):
            out_ref[span * PLACES + spot(place)] = jnp.zeros(out_ref.shape[1:], out_ref.dtype)
    copies[0].wait()
    for head in range(HEADS_HERE):
        cols = slice(head * HEAD_DIM, (head + 1) * HEAD_DIM)
        for block in range(BLOCKS):
            part = q_ref[block * QROWS : (block + 1) * QROWS, cols]
            for span in range(SPANS):
                out_ref[span * PLACES + spot(head * BLOCKS + block), :QROWS, :] = part
    copies[1].wait()
    copies[2].wait()
    key_rows = k_ref[...].astype(jnp.float32)
    value_rows = v_ref[...].astype(jnp.float32)
    for span in range(SPANS):
        kv_ref[span, :KROWS, :] = key_rows[span * KROWS : (span + 1) * KROWS]
        kv_ref[span, KROWS:, :] = value_rows[span * KROWS : (span + 1) * KROWS]
    for span in range(SPANS):
        both = kv_ref[span].astype(jnp.bfloat16)
        for head in range(HEADS_HERE):
            part = both[:, head * HEAD_DIM : (head + 1) * HEAD_DIM]
            for block in range(BLOCKS):
                out_ref[span * PLACES + spot(head * BLOCKS + block), QROWS:, :] = part


def split_three(x):
    high = x.astype(jnp.bfloat16)
    rest = x - high.astype(jnp.float32)
    middle = rest.astype(jnp.bfloat16)
    low = (rest - middle.astype(jnp.float32)).astype(jnp.bfloat16)
    return high, middle, low


def attend_kernel(order_ref, rows_ref, out_ref, keys_ref, values_ref):
    line = order_ref[...]
    order = [line[0, i] for i in range(SPANS)]
    spans = []
    for turn in range(SPANS):
        span = jnp.int32(0)
        for other in range(1, SPANS):
            span = span + jnp.where(order[other] == turn, other, 0)
        span = jnp.minimum(span, SPANS - 1)
        spans.append(span)
        for place in range(PLACES):
            both = rows_ref[span * PLACES + place, QROWS:, :].astype(jnp.float32)
            target = turn * KBLOCK + place * KROWS
            keys_ref[target : target + KROWS, :] = both[:KROWS]
            values_ref[target : target + KROWS, :] = both[KROWS:]
    keys = keys_ref[...].astype(jnp.bfloat16)
    values = values_ref[...].astype(jnp.bfloat16)
    state = []
    for turn, span in enumerate(spans):
        seen = (turn + 1) * KBLOCK
        own = jnp.concatenate(
            [rows_ref[span * PLACES + spot(place), :QROWS, :] for place in range(PLACES)], axis=0
        )
        scores = lax.dot_general(
            keys[:seen], own, (((1,), (1,)), ((), ())), preferred_element_type=jnp.float32
        )
        state.append(scores)
    soft = []
    for scores in state:
        highest = jnp.max(scores, axis=0, keepdims=True) * EXP2_SCALE
        weights = jnp.exp2(scores * EXP2_SCALE - highest)
        total = jnp.sum(weights, axis=0, keepdims=True)
        soft.append((highest, weights.astype(jnp.bfloat16), total))
    for turn, span in enumerate(spans):
        seen = (turn + 1) * KBLOCK
        highest, weights, total = soft[turn]
        mixed = lax.dot_general(
            weights, values[:seen], (((0,), (0,)), ((), ())), preferred_element_type=jnp.float32
        )
        mixed = (mixed * jnp.transpose(jnp.broadcast_to(1.0 / total, (HEAD_DIM, QBLOCK)))).astype(jnp.bfloat16)
        terms = [t.astype(jnp.float32) for t in split_three(highest + jnp.log2(total))]
        stat = [t[:, half * HEAD_DIM : (half + 1) * HEAD_DIM] for half in range(2) for t in terms]
        stat = jnp.concatenate(
            stat + [jnp.zeros((STATS - len(stat), HEAD_DIM), jnp.float32)], axis=0
        )
        for core in range(CORES):
            for ring in range(RING):
                source = (ring * CORES + core) * CHUNK
                out_ref[span * CORES + core, ring * CHUNK : (ring + 1) * CHUNK, :] = mixed[
                    source : source + CHUNK
                ]
            out_ref[span * CORES + core, RING * CHUNK :, :] = stat.astype(jnp.bfloat16)


def berth(place):
    return place // 4 * 4 + place % 2 * 2 + place // 2 % 2


def merge_kernel(parts_ref, out_ref, turn_ref):
    core = lax.axis_index("core")
    slots = (core, CORES - 1 - core)
    rows = []
    for half in range(2):
        for slot in slots:
            for s in range(SPANS):
                stats = parts_ref[s * CORES + slot, RING * CHUNK :, :].astype(jnp.float32)
                first = 3 * half
                rows.append(stats[first : first + 1] + stats[first + 1 : first + 2] + stats[first + 2 : first + 3])
    pad = jnp.zeros((HEAD_DIM - len(rows), HEAD_DIM), jnp.float32)
    turn_ref[...] = jnp.transpose(jnp.concatenate(rows + [pad], axis=0))
    for ring in range(RING):
        half, inner = divmod(ring, HEAD_DIM // (CORES * CHUNK))
        begin = pl.multiple_of((inner * CORES + core) * CHUNK, CHUNK)
        mine = turn_ref[pl.ds(begin, CHUNK), :]
        for i, slot in enumerate(slots):
            first = (half * CORES + i) * SPANS
            cols = [mine[:, first + s : first + s + 1] for s in range(SPANS)]
            highest = functools.reduce(jnp.maximum, cols)
            shares = [jnp.exp2(c - highest) for c in cols]
            total = functools.reduce(jnp.add, shares)
            mixed = jnp.zeros((CHUNK, HEAD_DIM), jnp.float32)
            for s in range(SPANS):
                part = parts_ref[s * CORES + slot, ring * CHUNK : (ring + 1) * CHUNK, :]
                mixed = mixed + part.astype(jnp.float32) * (shares[s] / total)
            mixed = mixed.astype(jnp.bfloat16)
            lanes = slice(i * HEAD_DIM, (i + 1) * HEAD_DIM)
            for place in range(PLACES):
                side = side_of(place)
                out_ref[berth(place), ring * QROWS : (ring + 1) * QROWS, lanes] = mixed[
                    side * QROWS : (side + 1) * QROWS
                ]


def project_kernel(rows_ref, own_ref, other_ref, theirs_ref, theirs_other_ref, out_ref):
    side = lax.axis_index("side")
    left = [
        jnp.concatenate(
            [
                jnp.concatenate(
                    [rows_ref[berth(head * BLOCKS + b), :, lanes] for b in range(BLOCKS)], axis=0
                )
                for head in range(HEADS_HERE)
            ],
            axis=1,
        )
        for lanes in (slice(0, HEAD_DIM), slice(HEAD_DIM, 2 * HEAD_DIM))
    ]
    for weights, target in (
        ((own_ref, other_ref), side),
        ((theirs_ref, theirs_other_ref), 1 - side),
    ):
        total = lax.dot_general(
            jnp.concatenate(left, axis=1),
            jnp.concatenate([w[...] for w in weights], axis=1),
            (((1,), (1,)), ((), ())),
            preferred_element_type=jnp.float32,
        )
        for ring in range(RING):
            piece = jnp.concatenate(
                [
                    total[(block * RING + ring) * QROWS : (block * RING + ring + 1) * QROWS]
                    for block in range(BLOCKS)
                ],
                axis=0,
            )
            edge = piece[:, 2 * HEAD_DIM :]
            edge = jnp.concatenate([edge[: ROWS // 2], edge[ROWS // 2 :]], axis=1)
            dense = [piece[:, :HEAD_DIM], piece[:, HEAD_DIM : 2 * HEAD_DIM], edge]
            out_ref[target * RING + ring] = jnp.concatenate(dense, axis=0).astype(jnp.bfloat16)


def finish_kernel(parts_ref, gate_ref, out_ref):
    gate = gate_ref[...]
    half, width = ROWS // 2, out_ref.shape[1] - 2 * HEAD_DIM
    for side in range(2):
        total = parts_ref[side * RING].astype(jnp.float32)
        for ring in range(1, RING):
            total = total + parts_ref[side * RING + ring].astype(jnp.float32)
        begin = side * ROWS
        for i in range(2):
            cols = slice(i * HEAD_DIM, (i + 1) * HEAD_DIM)
            part = total[i * ROWS : (i + 1) * ROWS] * gate[:, cols]
            out_ref[begin : begin + ROWS, cols] = part.astype(jnp.bfloat16)
        edge = total[2 * ROWS :]
        edge = jnp.concatenate([edge[:, :width], edge[:, width:]], axis=0) * gate[:, 2 * HEAD_DIM :]
        out_ref[begin : begin + ROWS, 2 * HEAD_DIM :] = edge.astype(jnp.bfloat16)


def side_of(place):
    return place // 2 % 2


def swap_sides(x):
    return lax.ppermute(x, "side", [(0, 1), (1, 0)])


def swap_cores(x):
    return lax.ppermute(x, "core", [(0, 1), (1, 0)])


def shards(queries, keys, values, out_weight, gate_table, noise_level, span_order):
    shard = (ROWS, HEADS_HERE * HEAD_DIM)
    packed = pl.pallas_call(
        pack_kernel,
        out_shape=jax.ShapeDtypeStruct((SPANS * PLACES, QROWS + 2 * KROWS, HEAD_DIM), jnp.bfloat16),
        in_specs=[HBM] * 3,
        out_specs=VMEM,
        scratch_shapes=[pltpu.VMEM(shard, jnp.bfloat16)] * 3
        + [
            pltpu.VMEM((SPANS, 2 * KROWS, shard[1]), jnp.float32),
            pltpu.SemaphoreType.DMA((3,)),
        ],
        compiler_params=params(60),
        name="pack",
    )(queries, keys, values)
    level = lax.dynamic_index_in_dim(noise_level, lax.axis_index("span"), 0, keepdims=False)
    gate_row = lax.dynamic_slice_in_dim(gate_table, level, 1, 0)
    packed, weight = lax.optimization_barrier((packed, out_weight.T))
    theirs, other = swap_sides(weight), swap_cores(weight)
    theirs_other = swap_cores(theirs)
    rows = lax.all_to_all(packed, ("span", "part", "far", "side"), 0, 0, tiled=True)
    parts = pl.pallas_call(
        attend_kernel,
        out_shape=jax.ShapeDtypeStruct((SPANS * CORES, RING * CHUNK + STATS, HEAD_DIM), jnp.bfloat16),
        in_specs=[VMEM, VMEM],
        out_specs=VMEM,
        scratch_shapes=[pltpu.VMEM((SPANS * KBLOCK, HEAD_DIM), jnp.float32)] * 2,
        compiler_params=params(),
        name="attend",
    )(span_order.reshape(1, SPANS), rows)
    parts, other, gate_row = lax.optimization_barrier((parts, other, gate_row))
    parts = lax.all_to_all(parts, ("span", "core"), 0, 0, tiled=True)
    parts, theirs, theirs_other = lax.optimization_barrier((parts, theirs, theirs_other))
    merged = pl.pallas_call(
        merge_kernel,
        out_shape=jax.ShapeDtypeStruct((PLACES, RING * QROWS, CORES * HEAD_DIM), jnp.bfloat16),
        in_specs=[VMEM],
        out_specs=VMEM,
        scratch_shapes=[pltpu.VMEM((HEAD_DIM, HEAD_DIM), jnp.float32)],
        compiler_params=params(),
        name="merge",
    )(parts)
    merged = lax.all_to_all(merged, ("far", "part", "side"), 0, 0, tiled=True)
    sums = pl.pallas_call(
        project_kernel,
        out_shape=jax.ShapeDtypeStruct((RING * 2, 2 * ROWS + ROWS // 2, HEAD_DIM), jnp.bfloat16),
        in_specs=[VMEM] * 5,
        out_specs=VMEM,
        compiler_params=params(),
        name="project",
    )(merged, weight, other, theirs, theirs_other)
    sums = lax.all_to_all(sums, ("side", "ring"), 0, 0, tiled=True)
    return pl.pallas_call(
        finish_kernel,
        out_shape=jax.ShapeDtypeStruct((2 * ROWS, out_weight.shape[1]), jnp.bfloat16),
        in_specs=[VMEM, VMEM],
        out_specs=VMEM,
        compiler_params=params(),
        name="finish",
    )(sums, gate_row)


def solution(mesh):
    fine = jax.sharding.Mesh(
        mesh.devices.reshape(SPANS, RING, CORES, 4, 2, 2),
        ("span", "ring", "core", "far", "side", "part"),
    )
    return jax.shard_map(
        shards,
        mesh=fine,
        in_specs=(
            P(("span",) + SEQ, HEAD),
            P(("span",) + SEQ, HEAD),
            P(("span",) + SEQ, HEAD),
            P(HEAD, SEQ),
            P(None, SEQ),
            P(),
            P(),
        ),
        out_specs=P(("span",) + HEAD, SEQ),
        check_vma=False,
    )
```

```python
import functools
import math

import jax
import jax.numpy as jnp
from jax import lax
from jax.experimental import pallas as pl
from jax.experimental.pallas import tpu as pltpu
from jax.sharding import PartitionSpec as P

HEAD_DIM = 128
SPANS = 4
RING, CORES = 4, 2
GROUPS = 8
HEADS_HERE = 5
BLOCKS = 3
PLACES = 16
ROWS = 48
QROWS = ROWS // BLOCKS
KROWS = ROWS // SPANS
KBLOCK = PLACES * KROWS
QBLOCK = PLACES * QROWS
CHUNK = 2 * QROWS
STATS = 8
HEAD = ("ring", "core")
SEQ = ("far", "side", "part")
EXP2_SCALE = math.log2(math.e) / math.sqrt(HEAD_DIM)
VMEM = pl.BlockSpec(memory_space=pltpu.VMEM)
HBM = pl.BlockSpec(memory_space=pltpu.HBM)


def params(mib=24):
    return pltpu.CompilerParams(vmem_limit_bytes=mib * 2**20)


def spot(place):
    return place % 2 * (PLACES // 2) + place // 2


def pack_kernel(q_hbm, k_hbm, v_hbm, out_ref, q_ref, k_ref, v_ref, kv_ref, sems):
    copies = [
        pltpu.make_async_copy(source, target, sems.at[i])
        for i, (source, target) in enumerate(((q_hbm, q_ref), (k_hbm, k_ref), (v_hbm, v_ref)))
    ]
    for copy in copies:
        copy.start()
    for span in range(SPANS):
        for place in range(HEADS_HERE * BLOCKS, PLACES):
            out_ref[span * PLACES + spot(place)] = jnp.zeros(out_ref.shape[1:], out_ref.dtype)
    copies[0].wait()
    for head in range(HEADS_HERE):
        cols = slice(head * HEAD_DIM, (head + 1) * HEAD_DIM)
        for block in range(BLOCKS):
            part = q_ref[block * QROWS : (block + 1) * QROWS, cols]
            for span in range(SPANS):
                out_ref[span * PLACES + spot(head * BLOCKS + block), :QROWS, :] = part
    copies[1].wait()
    copies[2].wait()
    key_rows = k_ref[...].astype(jnp.float32)
    value_rows = v_ref[...].astype(jnp.float32)
    for span in range(SPANS):
        kv_ref[span, :KROWS, :] = key_rows[span * KROWS : (span + 1) * KROWS]
        kv_ref[span, KROWS:, :] = value_rows[span * KROWS : (span + 1) * KROWS]
    for span in range(SPANS):
        both = kv_ref[span].astype(jnp.bfloat16)
        for head in range(HEADS_HERE):
            part = both[:, head * HEAD_DIM : (head + 1) * HEAD_DIM]
            for block in range(BLOCKS):
                out_ref[span * PLACES + spot(head * BLOCKS + block), QROWS:, :] = part


def split_three(x):
    high = x.astype(jnp.bfloat16)
    rest = x - high.astype(jnp.float32)
    middle = rest.astype(jnp.bfloat16)
    low = (rest - middle.astype(jnp.float32)).astype(jnp.bfloat16)
    return high, middle, low


def attend_kernel(order_ref, rows_ref, out_hbm, keys_ref, values_ref, out_ref, sems):
    line = order_ref[...]
    order = [line[0, i] for i in range(SPANS)]
    spans = []
    for turn in range(SPANS):
        span = jnp.int32(0)
        for other in range(1, SPANS):
            span = span + jnp.where(order[other] == turn, other, 0)
        span = jnp.minimum(span, SPANS - 1)
        spans.append(span)
        for place in range(PLACES):
            both = rows_ref[span * PLACES + place, QROWS:, :].astype(jnp.float32)
            target = turn * KBLOCK + place * KROWS
            keys_ref[target : target + KROWS, :] = both[:KROWS]
            values_ref[target : target + KROWS, :] = both[KROWS:]
    keys = keys_ref[...].astype(jnp.bfloat16)
    values = values_ref[...].astype(jnp.bfloat16)
    state, copies = [], []
    for turn, span in enumerate(spans):
        seen = (turn + 1) * KBLOCK
        own = jnp.concatenate(
            [rows_ref[span * PLACES + spot(place), :QROWS, :] for place in range(PLACES)], axis=0
        )
        scores = lax.dot_general(
            keys[:seen], own, (((1,), (1,)), ((), ())), preferred_element_type=jnp.float32
        )
        state.append(scores)
    soft = []
    for scores in state:
        highest = jnp.max(scores, axis=0, keepdims=True) * EXP2_SCALE
        weights = jnp.exp2(scores * EXP2_SCALE - highest)
        total = jnp.sum(weights, axis=0, keepdims=True)
        soft.append((highest, weights.astype(jnp.bfloat16), total))
    for turn, span in enumerate(spans):
        seen = (turn + 1) * KBLOCK
        highest, weights, total = soft[turn]
        mixed = lax.dot_general(
            weights, values[:seen], (((0,), (0,)), ((), ())), preferred_element_type=jnp.float32
        )
        mixed = (mixed * jnp.transpose(jnp.broadcast_to(1.0 / total, (HEAD_DIM, QBLOCK)))).astype(jnp.bfloat16)
        terms = [t.astype(jnp.float32) for t in split_three(highest + jnp.log2(total))]
        stat = [t[:, half * HEAD_DIM : (half + 1) * HEAD_DIM] for half in range(2) for t in terms]
        stat = jnp.concatenate(
            stat + [jnp.zeros((STATS - len(stat), HEAD_DIM), jnp.float32)], axis=0
        )
        for core in range(CORES):
            for ring in range(RING):
                source = (ring * CORES + core) * CHUNK
                out_ref[turn * CORES + core, ring * CHUNK : (ring + 1) * CHUNK, :] = mixed[
                    source : source + CHUNK
                ]
            out_ref[turn * CORES + core, RING * CHUNK :, :] = stat.astype(jnp.bfloat16)
            copies.append(
                pltpu.make_async_copy(
                    out_ref.at[turn * CORES + core],
                    out_hbm.at[core * SPANS + span],
                    sems.at[turn * CORES + core],
                )
            )
            copies[-1].start()
    for copy in copies:
        copy.wait()


def berth(place):
    return place // 4 * 4 + place % 2 * 2 + place // 2 % 2


def merge_kernel(parts_ref, out_ref, turn_ref):
    core = lax.axis_index("core")
    slots = (core, CORES - 1 - core)
    rows = []
    for half in range(2):
        for slot in slots:
            for s in range(SPANS):
                stats = parts_ref[slot * SPANS + s, RING * CHUNK :, :].astype(jnp.float32)
                first = 3 * half
                rows.append(stats[first : first + 1] + stats[first + 1 : first + 2] + stats[first + 2 : first + 3])
    pad = jnp.zeros((HEAD_DIM - len(rows), HEAD_DIM), jnp.float32)
    turn_ref[...] = jnp.transpose(jnp.concatenate(rows + [pad], axis=0))
    for ring in range(RING):
        half, inner = divmod(ring, HEAD_DIM // (CORES * CHUNK))
        begin = pl.multiple_of((inner * CORES + core) * CHUNK, CHUNK)
        mine = turn_ref[pl.ds(begin, CHUNK), :]
        for i, slot in enumerate(slots):
            first = (half * CORES + i) * SPANS
            cols = [mine[:, first + s : first + s + 1] for s in range(SPANS)]
            highest = functools.reduce(jnp.maximum, cols)
            shares = [jnp.exp2(c - highest) for c in cols]
            total = functools.reduce(jnp.add, shares)
            mixed = jnp.zeros((CHUNK, HEAD_DIM), jnp.float32)
            for s in range(SPANS):
                part = parts_ref[slot * SPANS + s, ring * CHUNK : (ring + 1) * CHUNK, :]
                mixed = mixed + part.astype(jnp.float32) * (shares[s] / total)
            mixed = mixed.astype(jnp.bfloat16)
            lanes = slice(i * HEAD_DIM, (i + 1) * HEAD_DIM)
            for place in range(PLACES):
                side = side_of(place)
                out_ref[berth(place), ring * QROWS : (ring + 1) * QROWS, lanes] = mixed[
                    side * QROWS : (side + 1) * QROWS
                ]


def project_kernel(rows_ref, own_ref, other_ref, theirs_ref, theirs_other_ref, out_ref):
    side = lax.axis_index("side")
    left = [
        jnp.concatenate(
            [
                jnp.concatenate(
                    [rows_ref[berth(head * BLOCKS + b), :, lanes] for b in range(BLOCKS)], axis=0
                )
                for head in range(HEADS_HERE)
            ],
            axis=1,
        )
        for lanes in (slice(0, HEAD_DIM), slice(HEAD_DIM, 2 * HEAD_DIM))
    ]
    for weights, target in (
        ((own_ref, other_ref), side),
        ((theirs_ref, theirs_other_ref), 1 - side),
    ):
        total = lax.dot_general(
            jnp.concatenate(left, axis=1),
            jnp.concatenate([w[...] for w in weights], axis=1),
            (((1,), (1,)), ((), ())),
            preferred_element_type=jnp.float32,
        )
        for ring in range(RING):
            piece = jnp.concatenate(
                [
                    total[(block * RING + ring) * QROWS : (block * RING + ring + 1) * QROWS]
                    for block in range(BLOCKS)
                ],
                axis=0,
            )
            edge = piece[:, 2 * HEAD_DIM :]
            edge = jnp.concatenate([edge[: ROWS // 2], edge[ROWS // 2 :]], axis=1)
            dense = [piece[:, :HEAD_DIM], piece[:, HEAD_DIM : 2 * HEAD_DIM], edge]
            out_ref[target * RING + ring] = jnp.concatenate(dense, axis=0).astype(jnp.bfloat16)


def finish_kernel(parts_ref, gate_ref, out_ref):
    gate = gate_ref[...]
    half, width = ROWS // 2, out_ref.shape[1] - 2 * HEAD_DIM
    for side in range(2):
        total = parts_ref[side * RING].astype(jnp.float32)
        for ring in range(1, RING):
            total = total + parts_ref[side * RING + ring].astype(jnp.float32)
        begin = side * ROWS
        for i in range(2):
            cols = slice(i * HEAD_DIM, (i + 1) * HEAD_DIM)
            part = total[i * ROWS : (i + 1) * ROWS] * gate[:, cols]
            out_ref[begin : begin + ROWS, cols] = part.astype(jnp.bfloat16)
        edge = total[2 * ROWS :]
        edge = jnp.concatenate([edge[:, :width], edge[:, width:]], axis=0) * gate[:, 2 * HEAD_DIM :]
        out_ref[begin : begin + ROWS, 2 * HEAD_DIM :] = edge.astype(jnp.bfloat16)


def side_of(place):
    return place // 2 % 2


def swap_sides(x):
    return lax.ppermute(x, "side", [(0, 1), (1, 0)])


def swap_cores(x):
    return lax.ppermute(x, "core", [(0, 1), (1, 0)])


def shards(queries, keys, values, out_weight, gate_table, noise_level, span_order):
    shard = (ROWS, HEADS_HERE * HEAD_DIM)
    packed = pl.pallas_call(
        pack_kernel,
        out_shape=jax.ShapeDtypeStruct((SPANS * PLACES, QROWS + 2 * KROWS, HEAD_DIM), jnp.bfloat16),
        in_specs=[HBM] * 3,
        out_specs=VMEM,
        scratch_shapes=[pltpu.VMEM(shard, jnp.bfloat16)] * 3
        + [
            pltpu.VMEM((SPANS, 2 * KROWS, shard[1]), jnp.float32),
            pltpu.SemaphoreType.DMA((3,)),
        ],
        compiler_params=params(60),
        name="pack",
    )(queries, keys, values)
    level = lax.dynamic_index_in_dim(noise_level, lax.axis_index("span"), 0, keepdims=False)
    gate_row = lax.dynamic_slice_in_dim(gate_table, level, 1, 0)
    packed, weight = lax.optimization_barrier((packed, out_weight.T))
    theirs, other = swap_sides(weight), swap_cores(weight)
    theirs_other = swap_cores(theirs)
    rows = lax.all_to_all(packed, ("span", "part", "far", "side"), 0, 0, tiled=True)
    parts = pl.pallas_call(
        attend_kernel,
        out_shape=jax.ShapeDtypeStruct((SPANS * CORES, RING * CHUNK + STATS, HEAD_DIM), jnp.bfloat16),
        in_specs=[VMEM, VMEM],
        out_specs=HBM,
        scratch_shapes=[pltpu.VMEM((SPANS * KBLOCK, HEAD_DIM), jnp.float32)] * 2
        + [
            pltpu.VMEM((SPANS * CORES, RING * CHUNK + STATS, HEAD_DIM), jnp.bfloat16),
            pltpu.SemaphoreType.DMA((SPANS * CORES,)),
        ],
        compiler_params=params(),
        name="attend",
    )(span_order.reshape(1, SPANS), rows)
    parts, other, gate_row = lax.optimization_barrier((parts, other, gate_row))
    parts = lax.all_to_all(parts, ("core", "span"), 0, 0, tiled=True)
    parts, theirs, theirs_other = lax.optimization_barrier((parts, theirs, theirs_other))
    merged = pl.pallas_call(
        merge_kernel,
        out_shape=jax.ShapeDtypeStruct((PLACES, RING * QROWS, CORES * HEAD_DIM), jnp.bfloat16),
        in_specs=[VMEM],
        out_specs=VMEM,
        scratch_shapes=[pltpu.VMEM((HEAD_DIM, HEAD_DIM), jnp.float32)],
        compiler_params=params(),
        name="merge",
    )(parts)
    merged = lax.all_to_all(merged, ("far", "part", "side"), 0, 0, tiled=True)
    sums = pl.pallas_call(
        project_kernel,
        out_shape=jax.ShapeDtypeStruct((RING * 2, 2 * ROWS + ROWS // 2, HEAD_DIM), jnp.bfloat16),
        in_specs=[VMEM] * 5,
        out_specs=VMEM,
        compiler_params=params(),
        name="project",
    )(merged, weight, other, theirs, theirs_other)
    sums = lax.all_to_all(sums, ("side", "ring"), 0, 0, tiled=True)
    return pl.pallas_call(
        finish_kernel,
        out_shape=jax.ShapeDtypeStruct((2 * ROWS, out_weight.shape[1]), jnp.bfloat16),
        in_specs=[VMEM, VMEM],
        out_specs=VMEM,
        compiler_params=params(),
        name="finish",
    )(sums, gate_row)


def solution(mesh):
    fine = jax.sharding.Mesh(
        mesh.devices.reshape(SPANS, RING, CORES, 4, 2, 2),
        ("span", "ring", "core", "far", "side", "part"),
    )
    return jax.shard_map(
        shards,
        mesh=fine,
        in_specs=(
            P(("span",) + SEQ, HEAD),
            P(("span",) + SEQ, HEAD),
            P(("span",) + SEQ, HEAD),
            P(HEAD, SEQ),
            P(None, SEQ),
            P(),
            P(),
        ),
        out_specs=P(("span",) + HEAD, SEQ),
        check_vma=False,
    )
```
